128 devices in a mesh: sess: 16 (over y_lo, z, core), tp: 8 (over y_hi, x).
Axes of the slice: x: 4, y: 4 (y_hi: 2, y_lo: 2; y = y_hi * 2 + y_lo), z: 4, core: 2. Of those that a mesh axis runs over, the one named last changes fastest.
Arguments:
- x_resid: bfloat16 [256, 8192], P(None, 'sess'), may hold values from -18 to 18
- qkv_new: bfloat16 [256, 8, 1280], P('sess', 'tp'), may hold values from -60 to 60
- kv_cache: bfloat16 [256, 2, 8, 1024, 128], P('sess', None, 'tp'), may hold values from -8 to 8
- cache_lens: int32 [256], P('sess'), may hold values from 1 to 1024, as said below
- wo_temporal: bfloat16 [8192, 8192], P('tp', 'sess'), may hold values from -0.0625 to 0.0625
- norm_gain: float32 [8192], P('sess'), may hold values from 0.1 to 1.9
- w_in: bfloat16 [8, 8192, 1024], P('tp', 'sess'), may hold values from -0.0625 to 0.0625
- embed_rows: bfloat16 [8, 2048, 1024], P('tp', 'sess'), may hold values from -6 to 6
- token_ids: int32 [256, 8], P(None, 'tp'), may hold values from 0 to 2047
- depth_gain: float32 [8, 1024], P('tp'), may hold values from 0.1 to 1.9
- depth_qkv: bfloat16 [8, 1024, 3072], P('tp'), may hold values from -6 to 6
- depth_out: bfloat16 [8, 1024, 1024], P('tp'), may hold values from -0.1875 to 0.1875
Outputs:
- depth_hidden: bfloat16 [256, 8, 1024], P('sess', 'tp')
The draws below stay inside these ranges and needn't reach their ends.
Inputs may be any that keep to these rules, and one draw needn't show every extreme that they name: `cache_lens`: some session has exactly 1024 live frames.
All inputs are finite; a program needn't handle non-finite values.
Results may differ from the reference program's by a relative error of at most 0.009.
Values may be sent and summed in bfloat16 or wider, within the bound.
A program may use at most 64 MiB of HBM per device.

```python
import math
import jax
import jax.numpy as jnp
from jax import lax

D = 8192
HQ = 64
KVH = 8
HD = 128
GROUP = 8
CACHE = 1024
SESSIONS = 256
NCB = 8
DDEP = 1024
DHEADS = 16
DH = 64
CARD = 2048


def draw_x_resid(key, part):
    first_key = jax.random.fold_in(jax.random.fold_in(key, 11), 0)
    third_key = jax.random.fold_in(jax.random.fold_in(key, 11), 2)
    ramp = jnp.exp(math.log(3.0) * jnp.arange(D, dtype=jnp.float32) / (D - 1))
    base = jnp.clip(jax.random.normal(first_key, (SESSIONS, D), jnp.float32), -6.0, 6.0)
    quiet = jax.random.randint(third_key, (SESSIONS, 1), 0, 4) == 0
    row_scale = jnp.where(quiet, 0.05, 1.0)
    return (base * ramp[None, :] * row_scale).astype(jnp.bfloat16)


def draw_qkv_new(key, part):
    first_key = jax.random.fold_in(jax.random.fold_in(key, 23), 0)
    width = (GROUP + 2) * HD
    base = jnp.clip(jax.random.normal(first_key, (SESSIONS, KVH, width), jnp.float32), -6.0, 6.0)
    return base.astype(jnp.bfloat16)


def draw_kv_cache(key, part):
    noise_key, offset_key = jax.random.split(jax.random.fold_in(key, 53))
    shape = (SESSIONS, 2, KVH, CACHE, HD)
    noise = jnp.clip(jax.random.normal(noise_key, shape, jnp.float32), -6.0, 6.0)
    offset = 0.4 * jnp.clip(jax.random.normal(offset_key, (SESSIONS, 1, KVH, 1, HD), jnp.float32), -3.0, 3.0)
    which = jnp.arange(2).reshape(1, 2, 1, 1, 1) == 1
    return (noise + jnp.where(which, offset, 0.0)).astype(jnp.bfloat16)


def draw_cache_lens(key, part):
    first_key, second_key = jax.random.split(jax.random.fold_in(key, 37))
    lengths = jax.random.randint(first_key, (SESSIONS,), 1, CACHE + 1)
    chosen = jax.random.randint(second_key, (), 0, SESSIONS)
    return lengths.at[chosen].set(CACHE).astype(jnp.int32)


def draw_depth_qkv(key, part):
    first_key = jax.random.fold_in(jax.random.fold_in(key, 41), 0)
    base = jnp.clip(jax.random.normal(first_key, (NCB, DDEP, 3 * DDEP), jnp.float32), -6.0, 6.0)
    base = base * DDEP ** (-0.5)
    return base.astype(jnp.bfloat16)


def plant(values, stream_key, smallest, largest):
    longest = values.shape.index(max(values.shape))
    spots = []
    for shift in (0, 1):
        where = [jax.random.randint(jax.random.fold_in(stream_key, axis), (), 0, length) for axis, length in enumerate(values.shape)]
        where[longest] = (where[longest] + shift) % values.shape[longest]
        spots.append(tuple(where))
    return values.at[spots[0]].set(smallest).at[spots[1]].set(largest)


def block_scale(key, shape, cuts, smallest, top_value):
    gain, own = 1.0, jax.random.fold_in(key, 6)
    for axis_at, parts in cuts:
        draws = jnp.exp(jax.random.uniform(jax.random.fold_in(own, axis_at), (parts,), jnp.float32, smallest / len(cuts), top_value / len(cuts)))
        gain = gain * jnp.repeat(draws, shape[axis_at] // parts).reshape([-1 if axis == axis_at else 1 for axis in range(len(shape))])
    return gain


def centred(own_key, dims, scale, most, cuts=(), held_as=jnp.bfloat16):
    values = scale * jax.random.normal(own_key, dims, jnp.float32)
    if cuts:
        values = values * block_scale(own_key, dims, cuts, -0.22, 0.18)
    return jnp.clip(values, -most, most).astype(held_as)


def setup_inputs(seed: int = 0) -> dict:
    seeds = jax.random.split(jax.random.key(seed), 13)
    x_resid = draw_x_resid(jax.random.fold_in(seeds[12], 71), 0)
    qkv_new = draw_qkv_new(jax.random.fold_in(seeds[12], 71), 0)
    kv_cache = draw_kv_cache(jax.random.fold_in(seeds[12], 71), 0)
    cache_lens = draw_cache_lens(jax.random.fold_in(seeds[12], 71), 0)
    wo_temporal = centred(seeds[4], (HQ * HD, D), (HQ * HD) ** -0.5, 0.0625, ((0, 8), (1, 16)))
    norm_gain = jnp.clip(1.0 + 0.18 * jax.random.normal(seeds[5], (D,), jnp.float32), 0.1, 1.9)
    w_in = centred(seeds[6], (NCB, D, DDEP), D ** -0.5, 0.0625, ((0, 8), (1, 16)))
    embed_rows = centred(seeds[7], (NCB, CARD, DDEP), 1.0, 6.0, ((0, 8), (1, 16)))
    token_ids = plant(jax.random.randint(seeds[8], (SESSIONS, NCB), 0, CARD), jax.random.fold_in(seeds[8], 1), 0, CARD - 1).astype(jnp.int32)
    depth_gain = jnp.clip(1.0 + 0.18 * jax.random.normal(seeds[9], (NCB, DDEP), jnp.float32), 0.1, 1.9)
    depth_qkv = draw_depth_qkv(jax.random.fold_in(seeds[12], 71), 0)
    depth_out = centred(seeds[11], (NCB, DDEP, DDEP), DDEP ** -0.5, 0.1875, ((0, 8),))
    return dict(x_resid=x_resid, qkv_new=qkv_new, kv_cache=kv_cache, cache_lens=cache_lens, wo_temporal=wo_temporal, norm_gain=norm_gain, w_in=w_in, embed_rows=embed_rows, token_ids=token_ids, depth_gain=depth_gain, depth_qkv=depth_qkv, depth_out=depth_out)


EPS = 1e-05

def attend_session(packed):
    joined, cache, length = packed
    group = joined.shape[1] // HD - 2
    queries = joined[:, :group * HD].astype(jnp.float32).reshape(KVH, group, HD)
    new_key = joined[:, group * HD:(group + 1) * HD].astype(jnp.float32)
    new_value = joined[:, (group + 1) * HD:].astype(jnp.float32)
    cache_f = cache.astype(jnp.float32)
    score_scale = HD ** (-0.5)
    old_scores = jnp.einsum('kgd,kld->kgl', queries, cache_f[0]) * score_scale
    new_scores = jnp.einsum('kgd,kd->kg', queries, new_key) * score_scale
    visible = jnp.arange(CACHE)[None, None, :] < length
    peak_score = jnp.maximum(lax.optimization_barrier(jnp.max(jnp.where(visible, old_scores, -1e+30), axis=-1)), new_scores)
    old_exp = jnp.where(visible, jnp.exp(old_scores - peak_score[..., None]), 0.0)
    new_exp = jnp.exp(new_scores - peak_score)
    summed_exp = lax.optimization_barrier(jnp.sum(old_exp, axis=-1)) + new_exp
    old_weights = (old_exp / summed_exp[..., None]).astype(jnp.bfloat16)
    new_weights = (new_exp / summed_exp).astype(jnp.bfloat16)
    context = jnp.einsum('kgl,kld->kgd', old_weights.astype(jnp.float32), cache_f[1])
    context = context + new_weights.astype(jnp.float32)[..., None] * new_value[:, None, :]
    return context.astype(jnp.bfloat16).reshape(KVH * group * HD)

def reference(x_resid, qkv_new, kv_cache, cache_lens, wo_temporal, norm_gain, w_in, embed_rows, token_ids, depth_gain, depth_qkv, depth_out):
    attn = lax.map(attend_session, (qkv_new, kv_cache, cache_lens))
    temporal = jnp.dot(attn, wo_temporal, preferred_element_type=jnp.float32)
    hidden = x_resid.astype(jnp.float32) + temporal
    squares = lax.optimization_barrier(jnp.sum(hidden * hidden, axis=1))
    normed = (hidden * lax.rsqrt(squares / D + EPS)[:, None] * norm_gain.astype(jnp.float32)[None, :]).astype(jnp.bfloat16)
    looked = embed_rows[jnp.arange(NCB)[None, :], token_ids].astype(jnp.float32)
    depth_in = jnp.einsum('sd,cde->sce', normed.astype(jnp.float32), w_in.astype(jnp.float32)) + looked
    mean_sq = lax.optimization_barrier(jnp.mean(depth_in * depth_in, axis=-1))
    depth_normed = (depth_in * lax.rsqrt(mean_sq + EPS)[..., None] * depth_gain.astype(jnp.float32)[None]).astype(jnp.bfloat16)
    depth_proj = jnp.einsum('sce,cef->scf', depth_normed.astype(jnp.float32), depth_qkv.astype(jnp.float32)).astype(jnp.bfloat16)
    rows = depth_proj.shape[0]
    queries = depth_proj[..., :DDEP].astype(jnp.float32).reshape(rows, NCB, DHEADS, DH)
    keys = depth_proj[..., DDEP:2 * DDEP].astype(jnp.float32).reshape(rows, NCB, DHEADS, DH)
    values = depth_proj[..., 2 * DDEP:].astype(jnp.float32).reshape(rows, NCB, DHEADS, DH)
    scores = jnp.einsum('schd,skhd->schk', queries, keys) * DH ** (-0.5)
    causal = jnp.arange(NCB)[None, :] <= jnp.arange(NCB)[:, None]
    causal = causal[None, :, None, :]
    peak_score = lax.optimization_barrier(jnp.max(jnp.where(causal, scores, -1e+30), axis=-1))
    expo = jnp.where(causal, jnp.exp(scores - peak_score[..., None]), 0.0)
    probs = expo / lax.optimization_barrier(jnp.sum(expo, axis=-1))[..., None]
    depth_ctx = jnp.einsum('schk,skhd->schd', probs, values).reshape(rows, NCB, DDEP).astype(jnp.bfloat16)
    projected = jnp.einsum('sce,cef->scf', depth_ctx.astype(jnp.float32), depth_out.astype(jnp.float32))
    return (depth_in + projected).astype(jnp.bfloat16)
```

```python
import jax
import jax.numpy as jnp
from jax import lax
from jax.experimental import pallas as pl
from jax.experimental.pallas import tpu as pltpu
from jax.sharding import PartitionSpec as P

MESH = pl.DeviceIdType.MESH
F32 = jnp.float32
BF16 = jnp.bfloat16

D = 8192
EPS = 1e-05
CHIPS = 8
TP = 8
ROWS = 16
GROUP = 8
HD = 128
FRAMES = 1024
COLS = 512
DDEP = 1024
WIDE = DDEP + 128
PAIR = 128
DH = 64
SESS_PER_STEP = 4


def nt_dot(a, b):
    return lax.dot_general(a, b, (((1,), (1,)), ((), ())), preferred_element_type=F32)


def dot(a, b):
    return jnp.dot(a, b, preferred_element_type=F32)


def frame_kernel(
    x_hbm,
    qkv_hbm,
    kv_hbm,
    lens_hbm,
    wo_hbm,
    gain_hbm,
    win_hbm,
    emb_hbm,
    tok_hbm,
    dgain_hbm,
    dqkv_hbm,
    dout_hbm,
    out_ref,
    kv,
    wo,
    win,
    emb,
    dqkv,
    dout,
    xres,
    qkv,
    lens,
    gain,
    dgain,
    tok,
    kv_sem,
    in_sem,
    q_scr,
    o_scr,
    attn_all,
    part,
    part_in,
    hid_all,
    onehot,
    look_sib,
    look_in_sib,
    look_out,
    look_in,
    c_sib,
    c_in_sib,
    c_own,
    c_out,
    c_in,
    d_out,
    d_in,
    e_out,
    e_in,
    a_send,
    a_recv,
    as_send,
    as_recv,
    b_send,
    b_recv,
    h_send,
    h_recv,
    c_send,
    c_recv,
    d_send,
    d_recv,
    e_send,
    e_recv,
    l_send,
    l_recv,
    sib_send,
    sib_recv,
):
    s = lax.axis_index("sess")
    t = lax.axis_index("tp")
    chip = s // 2
    core = s % 2
    other = 1 - core
    sibling = (chip * 2 + other, t)

    def chip_at(d):
        return ((chip // 4 + d // 4) % 2) * 4 + (chip % 4 + d % 4) % 4

    def chip_from(d):
        return ((chip // 4 + d // 4) % 2) * 4 + (chip % 4 + 4 - d % 4) % 4

    def tp_at(d):
        return ((t // 4 + d // 4) % 2) * 4 + (t % 4 + d % 4) % 4

    def tp_from(d):
        return ((t // 4 + d // 4) % 2) * 4 + (t % 4 + 4 - d % 4) % 4

    def remote(src, dst, send, recv, device):
        return pltpu.make_async_remote_copy(
            src_ref=src,
            dst_ref=dst,
            send_sem=send,
            recv_sem=recv,
            device_id=device,
            device_id_type=MESH,
        )

    def load(i, src, dst):
        return pltpu.make_async_copy(src, dst, in_sem.at[i])

    x_load = load(0, x_hbm.at[pl.ds(pl.multiple_of(t * 32, 32), 32)], xres)
    qkv_load = load(1, qkv_hbm, qkv)
    lens_load = load(2, lens_hbm, lens)
    gain_load = load(3, gain_hbm, gain)
    dgain_load = load(4, dgain_hbm, dgain)
    tok_load = load(5, tok_hbm, tok)
    emb_load = load(6, emb_hbm, emb)
    wo_load = load(7, wo_hbm, wo)
    win_load = load(8, win_hbm, win)
    dqkv_load = load(9, dqkv_hbm, dqkv)
    dout_load = load(10, dout_hbm, dout)
    kv_loads = [pltpu.make_async_copy(kv_hbm.at[i], kv.at[i], kv_sem.at[i]) for i in range(ROWS)]

    qkv_load.start()
    lens_load.start()
    for copy in kv_loads[:8]:
        copy.start()
    tok_load.start()
    emb_load.start()
    for copy in kv_loads[8:]:
        copy.start()
    gain_load.start()
    dgain_load.start()
    x_load.start()

    barrier = pltpu.get_barrier_semaphore()
    pl.semaphore_signal(barrier, inc=1, device_id=sibling, device_id_type=MESH)
    for d in range(1, CHIPS):
        pl.semaphore_signal(barrier, inc=1, device_id=(chip_at(d) * 2 + core, t), device_id_type=MESH)
        pl.semaphore_signal(barrier, inc=1, device_id=(s, tp_at(d)), device_id_type=MESH)

    qkv_load.wait()
    lens_load.wait()
    for h in range(GROUP):
        q_scr[pl.ds(h, ROWS, stride=GROUP), :] = qkv[:, h * HD : (h + 1) * HD].astype(F32)
    scale = HD ** (-0.5)
    frame = lax.broadcasted_iota(jnp.int32, (GROUP, FRAMES), 1)

    def attend(i):
        q = q_scr[i * GROUP : (i + 1) * GROUP, :]
        new_key = qkv[i : i + 1, GROUP * HD : (GROUP + 1) * HD].astype(F32)
        new_value = qkv[i : i + 1, (GROUP + 1) * HD :].astype(F32)
        new_score = jnp.sum(q * new_key, axis=1, keepdims=True) * scale
        scores = nt_dot(q.astype(BF16), kv[i, 0]) * scale
        scores = jnp.where(frame < lens[i], scores, -1e30)
        peak = jnp.maximum(jnp.max(scores, axis=1, keepdims=True), new_score)
        expo = jnp.exp(scores - peak)
        new_expo = jnp.exp(new_score - peak)
        inv = 1.0 / (jnp.sum(expo, axis=1, keepdims=True) + new_expo)
        weights = (expo * inv).astype(BF16)
        new_weight = (new_expo * inv).astype(BF16).astype(F32)
        o_scr[i * GROUP : (i + 1) * GROUP, :] = dot(weights, kv[i, 1]) + new_weight * new_value

    def attend_step(g):
        for i in range(g * SESS_PER_STEP, (g + 1) * SESS_PER_STEP):
            kv_loads[i].wait()
        for i in range(g * SESS_PER_STEP, (g + 1) * SESS_PER_STEP):
            attend(i)

    attend_step(0)

    tok_load.wait()
    emb_load.wait()
    entry = lax.broadcasted_iota(jnp.int32, (128, 256), 0) + s * 128
    hot = jnp.where(tok[...] == entry, 1.0, 0.0).T.astype(BF16)
    onehot[...] = hot.reshape(CHIPS, 2, ROWS, 128)
    hot_other = onehot[:, pl.ds(other, 1)].reshape(CHIPS * ROWS, 128)
    look_sib[...] = dot(hot_other, emb[...]).astype(BF16).reshape(CHIPS, ROWS, DDEP)
    pl.semaphore_wait(barrier, 15)
    look_to_sib = remote(look_sib, look_in_sib, sib_send.at[0], sib_recv.at[0], sibling)
    look_to_sib.start()

    attend_step(1)

    hot_own = onehot[:, pl.ds(core, 1)].reshape(CHIPS * ROWS, 128)
    look_to_sib.wait()
    look_out[...] = (
        dot(hot_own, emb[...]).reshape(CHIPS, ROWS, DDEP) + look_in_sib[...].astype(F32)
    ).astype(BF16)
    look_copies = []
    for d in range(1, CHIPS):
        to = chip_at(d)
        copy = remote(look_out.at[to], look_in.at[d], l_send.at[d], l_recv.at[d], (to * 2 + core, t))
        copy.start()
        look_copies.append(copy)

    attend_step(2)
    wo_load.start()
    win_load.start()
    attend_step(3)
    dqkv_load.start()
    dout_load.start()

    for h in range(GROUP):
        attn_all[chip, core, :, h * HD : (h + 1) * HD] = o_scr[pl.ds(h, ROWS, stride=GROUP), :].astype(BF16)
    mine = attn_all.at[chip, core]
    gather = []
    for d in range(1, CHIPS):
        copy = remote(mine, mine, a_send.at[d], a_recv.at[d], (chip_at(d) * 2 + core, t))
        copy.start()
        gather.append(copy)
    across = [remote(mine, mine, as_send.at[0], as_recv.at[0], sibling)]
    across[0].start()

    gain_load.wait()
    win_load.wait()
    gain_col = jnp.broadcast_to(gain[...], (128, COLS)).T
    for j in range(DDEP // 128):
        cols = slice(j * 128, (j + 1) * 128)
        win[:, cols] = (win[:, cols].astype(F32) * gain_col).astype(BF16)

    for d in range(1, CHIPS):
        gather[d - 1].wait_recv()
        block = attn_all.at[chip_from(d), core]
        copy = remote(block, block, as_send.at[d], as_recv.at[d], sibling)
        copy.start()
        across.append(copy)
    wo_load.wait()
    for copy in across:
        copy.wait_recv()

    for q in range(2):
        rows = attn_all[q * 4 : (q + 1) * 4].reshape(128, GROUP * HD)
        part[q * 4 : (q + 1) * 4] = dot(rows, wo[...]).astype(BF16).reshape(4, 32, COLS)
    reduce_tp = []
    for d in range(1, TP):
        to = tp_at(d)
        copy = remote(part.at[to], part_in.at[d], b_send.at[d], b_recv.at[d], (s, to))
        copy.start()
        reduce_tp.append(copy)
    x_load.wait()
    hidden = xres[...].astype(F32) + part[t].astype(F32)
    for d in range(1, TP):
        reduce_tp[d - 1].wait_recv()
        hidden = hidden + part_in[d].astype(F32)
    hid_all[t] = hidden.astype(BF16).reshape(2, ROWS, COLS)
    my_hidden = hid_all.at[t]
    gather_tp = []
    for d in range(1, TP):
        copy = remote(my_hidden, my_hidden, h_send.at[d], h_recv.at[d], (s, tp_at(d)))
        copy.start()
        gather_tp.append(copy)
    for copy in gather_tp:
        copy.wait_recv()

    lane = lax.broadcasted_iota(jnp.int32, (CHIPS * ROWS, 128), 1)

    def project(parity):
        rows = hid_all[:, pl.ds(parity, 1)].reshape(CHIPS * ROWS, COLS)
        wide = rows.astype(F32)
        squares = jnp.sum(wide * wide, axis=1, keepdims=True)
        high = squares.astype(BF16).astype(F32)
        low = squares - high
        extra = jnp.where(lane == 2 * core, high, 0.0) + jnp.where(lane == 2 * core + 1, low, 0.0)
        return dot(rows, win[...]).reshape(CHIPS, ROWS, DDEP), extra.reshape(CHIPS, ROWS, 128)

    product, extra = project(other)
    c_sib[:, :, :DDEP] = product.astype(BF16)
    c_sib[:, :, DDEP:] = extra.astype(BF16)
    to_sib = remote(c_sib, c_in_sib, sib_send.at[1], sib_recv.at[1], sibling)
    to_sib.start()
    product, extra = project(core)
    c_own[:, :, :DDEP] = product
    c_own[:, :, DDEP:] = extra
    to_sib.wait()
    c_out[...] = (c_own[...] + c_in_sib[...].astype(F32)).astype(BF16)
    reduce_sess = []
    for d in range(1, CHIPS):
        to = chip_at(d)
        copy = remote(c_out.at[to], c_in.at[d], c_send.at[d], c_recv.at[d], (to * 2 + core, t))
        copy.start()
        reduce_sess.append(copy)
    looked = look_out[chip].astype(F32)
    for d in range(1, CHIPS):
        look_copies[d - 1].wait_recv()
        looked = looked + look_in[d].astype(F32)
    summed = c_out[chip].astype(F32)
    for d in range(1, CHIPS):
        reduce_sess[d - 1].wait_recv()
        summed = summed + c_in[d].astype(F32)
    squares = jnp.sum(summed[:, DDEP:], axis=1, keepdims=True)
    depth_in = summed[:, :DDEP] * lax.rsqrt(squares / D + EPS) + looked

    dgain_load.wait()
    mean_sq = jnp.mean(depth_in * depth_in, axis=1, keepdims=True)
    normed = (depth_in * lax.rsqrt(mean_sq + EPS) * dgain[...]).astype(BF16)
    dqkv_load.wait()
    for u in range(4):
        for p in range(3):
            first = p * DDEP + u * 256
            y = dot(normed, dqkv[:, first : first + 256]).astype(BF16)
            d_out[2 * u, :, p * PAIR : (p + 1) * PAIR] = y[:, :PAIR]
            d_out[2 * u + 1, :, p * PAIR : (p + 1) * PAIR] = y[:, PAIR:]
    heads_out = []
    for d in range(1, TP):
        to = tp_at(d)
        copy = remote(d_out.at[to], d_in.at[t], d_send.at[d], d_recv.at[d], (s, to))
        copy.start()
        heads_out.append(copy)
    d_in[t] = d_out[t]
    for copy in heads_out:
        copy.wait_recv()

    qs = [d_in[c, :, :PAIR].astype(F32) for c in range(TP)]
    ks = [d_in[c, :, PAIR : 2 * PAIR].astype(F32) for c in range(TP)]
    vs = [d_in[c, :, 2 * PAIR :].astype(F32) for c in range(TP)]
    products = jnp.concatenate([qs[c] * ks[j] for c in range(TP) for j in range(c + 1)], axis=0)
    high = products.astype(BF16)
    low = (products - high.astype(F32)).astype(BF16)
    half_r = lax.broadcasted_iota(jnp.int32, (PAIR, PAIR), 0) // DH
    half_c = lax.broadcasted_iota(jnp.int32, (PAIR, PAIR), 1) // DH
    same_head = jnp.where(half_r == half_c, 1.0, 0.0).astype(BF16)
    scores = (dot(high, same_head) + dot(low, same_head)) * DH ** (-0.5)
    at = 0
    for c in range(TP):
        rows = [scores[(at + j) * ROWS : (at + j + 1) * ROWS] for j in range(c + 1)]
        at += c + 1
        peak = rows[0]
        for row in rows[1:]:
            peak = jnp.maximum(peak, row)
        total = jnp.zeros((ROWS, PAIR), F32)
        context = jnp.zeros((ROWS, PAIR), F32)
        for j, row in enumerate(rows):
            weight = jnp.exp(row - peak)
            total = total + weight
            context = context + weight * vs[j]
        e_out[c] = (context / total).astype(BF16)
    heads_back = []
    for d in range(1, TP):
        to = tp_at(d)
        copy = remote(e_out.at[to], e_in.at[t], e_send.at[d], e_recv.at[d], (s, to))
        copy.start()
        heads_back.append(copy)
    e_in[t] = e_out[t]
    dout_load.wait()
    for copy in heads_back:
        copy.wait_recv()
    context = jnp.concatenate([e_in[c] for c in range(TP)], axis=1)
    out_ref[...] = (depth_in + dot(context, dout[...])).astype(BF16)

    for copy in gather + across + reduce_tp + gather_tp + reduce_sess + look_copies + heads_out + heads_back:
        copy.wait_send()


def shards(
    x_resid,
    qkv_new,
    kv_cache,
    cache_lens,
    wo_temporal,
    norm_gain,
    w_in,
    embed_rows,
    token_ids,
    depth_gain,
    depth_qkv,
    depth_out,
):
    args = (
        x_resid,
        qkv_new.reshape(ROWS, (GROUP + 2) * HD),
        kv_cache.reshape(ROWS, 2, FRAMES, HD),
        cache_lens,
        wo_temporal,
        norm_gain.reshape(1, COLS),
        w_in.reshape(COLS, DDEP),
        embed_rows.reshape(128, DDEP),
        token_ids.reshape(1, 256),
        depth_gain,
        depth_qkv.reshape(DDEP, 3 * DDEP),
        depth_out.reshape(DDEP, DDEP),
    )
    dma = pltpu.SemaphoreType.DMA
    vm = pltpu.VMEM
    out = pl.pallas_call(
        frame_kernel,
        name="frame",
        out_shape=jax.ShapeDtypeStruct((ROWS, DDEP), BF16),
        in_specs=[pl.BlockSpec(memory_space=pl.ANY)] * len(args),
        out_specs=pl.BlockSpec(memory_space=pltpu.VMEM),
        scratch_shapes=[
            vm((ROWS, 2, FRAMES, HD), BF16),
            vm((GROUP * HD, COLS), BF16),
            vm((COLS, DDEP), BF16),
            vm((128, DDEP), BF16),
            vm((DDEP, 3 * DDEP), BF16),
            vm((DDEP, DDEP), BF16),
            vm((32, COLS), BF16),
            vm((ROWS, (GROUP + 2) * HD), BF16),
            pltpu.SMEM((ROWS,), jnp.int32),
            vm((1, COLS), F32),
            vm((1, DDEP), F32),
            vm((1, 256), jnp.int32),
            dma((ROWS,)),
            dma((11,)),
            vm((ROWS * GROUP, HD), F32),
            vm((ROWS * GROUP, HD), F32),
            vm((CHIPS, 2, ROWS, GROUP * HD), BF16),
            vm((TP, 32, COLS), BF16),
            vm((TP, 32, COLS), BF16),
            vm((TP, 2, ROWS, COLS), BF16),
            vm((CHIPS, 2, ROWS, 128), BF16),
            vm((CHIPS, ROWS, DDEP), BF16),
            vm((CHIPS, ROWS, DDEP), BF16),
            vm((CHIPS, ROWS, DDEP), BF16),
            vm((CHIPS, ROWS, DDEP), BF16),
            vm((CHIPS, ROWS, WIDE), BF16),
            vm((CHIPS, ROWS, WIDE), BF16),
            vm((CHIPS, ROWS, WIDE), F32),
            vm((CHIPS, ROWS, WIDE), BF16),
            vm((CHIPS, ROWS, WIDE), BF16),
            vm((TP, ROWS, 3 * PAIR), BF16),
            vm((TP, ROWS, 3 * PAIR), BF16),
            vm((TP, ROWS, PAIR), BF16),
            vm((TP, ROWS, PAIR), BF16),
            dma((8,)),
            dma((8,)),
            dma((8,)),
            dma((8,)),
            dma((8,)),
            dma((8,)),
            dma((8,)),
            dma((8,)),
            dma((8,)),
            dma((8,)),
            dma((8,)),
            dma((8,)),
            dma((8,)),
            dma((8,)),
            dma((8,)),
            dma((8,)),
            dma((2,)),
            dma((2,)),
        ],
        compiler_params=pltpu.CompilerParams(
            collective_id=0, has_side_effects=True, vmem_limit_bytes=48 * 2**20
        ),
        cost_estimate=pl.CostEstimate(flops=10**9, bytes_accessed=19 * 10**6, transcendentals=10**5),
    )(*args)
    return out.reshape(ROWS, 1, DDEP)


def solution(mesh):
    in_specs = (
        P(None, "sess"),
        P("sess", "tp", None),
        P("sess", None, "tp", None, None),
        P("sess"),
        P("tp", "sess"),
        P("sess"),
        P("tp", "sess", None),
        P("tp", "sess", None),
        P(None, "tp"),
        P("tp", None),
        P("tp", None, None),
        P("tp", None, None),
    )
    out_specs = P("sess", "tp", None)
    return jax.shard_map(shards, mesh=mesh, in_specs=in_specs, out_specs=out_specs, check_vma=False)
```

```python
import jax
import jax.numpy as jnp
from jax import lax
from jax.experimental import pallas as pl
from jax.experimental.pallas import tpu as pltpu
from jax.sharding import PartitionSpec as P

MESH = pl.DeviceIdType.MESH
F32 = jnp.float32
BF16 = jnp.bfloat16

D = 8192
EPS = 1e-05
CHIPS = 8
TP = 8
ROWS = 16
GROUP = 8
HD = 128
FRAMES = 1024
COLS = 512
DDEP = 1024
WIDE = DDEP + 128
QUAD = 256
DH = 64
STEP = 4


def dot(a, b):
    return jnp.dot(a, b, preferred_element_type=F32)


def frame_kernel(
    x_hbm,
    qkv_hbm,
    kv_hbm,
    lens_hbm,
    wo_hbm,
    gain_hbm,
    win_hbm,
    emb_hbm,
    tok_hbm,
    dgain_hbm,
    dqkv_hbm,
    dout_hbm,
    out_ref,
    keys,
    values,
    wo,
    win,
    emb,
    dqkv,
    dout,
    xres,
    qkv,
    lens,
    gain,
    dgain,
    tok,
    kv_sem,
    in_sem,
    q_scr,
    k_scr,
    v_scr,
    query_cols,
    score_scr,
    weight_scr,
    o_scr,
    attn_all,
    part,
    part_in,
    hid_all,
    onehot,
    look_own,
    look_sib,
    look_in_sib,
    look_out,
    look_in,
    c_sib,
    c_in_sib,
    c_out,
    c_in,
    d_out,
    d_in,
    e_out,
    e_in,
    a_send,
    a_recv,
    f_send,
    f_recv,
    b_send,
    b_recv,
    h_send,
    h_recv,
    c_send,
    c_recv,
    d_send,
    d_recv,
    e_send,
    e_recv,
    l_send,
    l_recv,
    sib_send,
    sib_recv,
):
    s = lax.axis_index("sess")
    t = lax.axis_index("tp")
    chip = s // 2
    core = s % 2
    other = 1 - core
    row = t // 4
    col = t % 4
    sibling = (chip * 2 + other, t)

    def step_of(d):
        return ((0, 1), (0, 3), (1, 0), (0, 2), (1, 1), (1, 3), (1, 2))[d - 1]

    def at(i, d):
        hi, lo = step_of(d)
        return ((i // 4 + hi) % 2) * 4 + (i % 4 + lo) % 4

    def back(i, d):
        hi, lo = step_of(d)
        return ((i // 4 + hi) % 2) * 4 + (i % 4 + 4 - lo) % 4

    far_first = (7, 6, 5, 4, 3, 2, 1)
    near_first = (1, 2, 3, 4, 5, 6, 7)

    def remote(src, dst, send, recv, device):
        return pltpu.make_async_remote_copy(
            src_ref=src,
            dst_ref=dst,
            send_sem=send,
            recv_sem=recv,
            device_id=device,
            device_id_type=MESH,
        )

    def load(i, src, dst):
        return pltpu.make_async_copy(src, dst, in_sem.at[i])

    x_load = load(0, x_hbm.at[pl.ds(pl.multiple_of(t * 32, 32), 32)], xres)
    qkv_load = load(1, qkv_hbm, qkv)
    lens_load = load(2, lens_hbm, lens)
    gain_load = load(3, gain_hbm, gain)
    dgain_load = load(4, dgain_hbm, dgain)
    tok_load = load(5, tok_hbm, tok)
    emb_load = load(6, emb_hbm, emb)
    wo_load = load(7, wo_hbm, wo)
    win_load = load(8, win_hbm, win)
    dqkv_load = load(9, dqkv_hbm, dqkv)
    dout_load = load(10, dout_hbm, dout)
    key_loads = [
        pltpu.make_async_copy(kv_hbm.at[pl.ds(g * STEP, STEP), 0], keys.at[pl.ds(g * STEP, STEP)], kv_sem.at[0, g])
        for g in range(ROWS // STEP)
    ]
    value_loads = [
        pltpu.make_async_copy(kv_hbm.at[pl.ds(g * STEP, STEP), 1], values.at[pl.ds(g * STEP, STEP)], kv_sem.at[1, g])
        for g in range(ROWS // STEP)
    ]
    for copy in [qkv_load, lens_load, tok_load, emb_load] + key_loads + value_loads:
        copy.start()
    for copy in (gain_load, dgain_load, x_load):
        copy.start()

    barrier = pltpu.get_barrier_semaphore()
    pl.semaphore_signal(barrier, inc=1, device_id=sibling, device_id_type=MESH)
    for d in near_first:
        for device in ((at(chip, d) * 2, t), (at(chip, d) * 2 + 1, t), (s, at(t, d))):
            pl.semaphore_signal(barrier, inc=1, device_id=device, device_id_type=MESH)

    qkv_load.wait()
    new_keys = qkv[:, GROUP * HD : (GROUP + 1) * HD].astype(F32)
    new_values = qkv[:, (GROUP + 1) * HD :].astype(F32)
    for h in range(GROUP):
        rows_h = pl.ds(h, ROWS, stride=GROUP)
        q_scr[rows_h, :] = qkv[:, h * HD : (h + 1) * HD].astype(F32)
        k_scr[rows_h, :] = new_keys
        v_scr[rows_h, :] = new_values
    query_t = q_scr[...].T
    scale = HD ** (-0.5)
    new_score = jnp.sum(query_t * k_scr[...].T, axis=0, keepdims=True) * scale
    owner = lax.broadcasted_iota(jnp.int32, (HD, HD), 1) // GROUP
    for i in range(ROWS):
        query_cols[i * HD : (i + 1) * HD, :] = jnp.where(owner == i, query_t, 0.0).astype(BF16)
    lens_load.wait()
    owner_row = lax.broadcasted_iota(jnp.int32, (1, HD), 1) // GROUP
    live = jnp.zeros((1, HD), jnp.int32)
    for i in range(ROWS):
        live = jnp.where(owner_row == i, lens[i], live)

    tok_load.wait()
    emb_load.wait()
    entry = lax.broadcasted_iota(jnp.int32, (128, 256), 0) + s * 128
    hot = jnp.where(tok[...] == entry, 1.0, 0.0).T.astype(BF16)
    onehot[...] = hot.reshape(CHIPS, 2, ROWS, 128)

    def look(parity):
        rows = onehot[:, pl.ds(parity, 1)].reshape(CHIPS * ROWS, 128)
        return dot(rows, emb[...]).astype(BF16).reshape(CHIPS, ROWS, DDEP)

    look_sib[...] = look(other)
    look_own[...] = look(core)

    for g in range(ROWS // STEP):
        key_loads[g].wait()
        joined = jnp.concatenate([keys[g * STEP + i] for i in range(STEP)], axis=1)
        scores = dot(joined, query_cols[g * STEP * HD : (g + 1) * STEP * HD, :])
        if g == 0:
            score_scr[...] = scores
        else:
            score_scr[...] += scores
    wo_load.start()
    win_load.start()
    pl.semaphore_wait(barrier, 22)
    look_to_sib = remote(look_sib, look_in_sib, sib_send.at[0], sib_recv.at[0], sibling)
    look_to_sib.start()

    frame = lax.broadcasted_iota(jnp.int32, (FRAMES, HD), 0)
    masked = jnp.where(frame < live, score_scr[...] * scale, -1e30)
    peak = jnp.maximum(jnp.max(masked, axis=0, keepdims=True), new_score)
    expo = jnp.exp(masked - peak)
    new_expo = jnp.exp(new_score - peak)
    inv = 1.0 / (jnp.sum(expo, axis=0, keepdims=True) + new_expo)
    weight_scr[...] = (expo * inv).T
    new_weight = (new_expo * inv).astype(BF16).astype(F32)
    o_scr[...] = jnp.broadcast_to(new_weight, (HD, HD)).T * v_scr[...]
    for g in range(ROWS // STEP):
        value_loads[g].wait()
        for i in range(g * STEP, (g + 1) * STEP):
            rows_i = slice(i * GROUP, (i + 1) * GROUP)
            o_scr[rows_i, :] += dot(weight_scr[rows_i, :].astype(BF16), values[i])
    dqkv_load.start()
    dout_load.start()

    for h in range(GROUP):
        attn_all[chip, core, :, h * HD : (h + 1) * HD] = o_scr[pl.ds(h, ROWS, stride=GROUP), :].astype(BF16)
    mine = attn_all.at[chip, core]
    gather = {}
    for d in far_first:
        gather[d] = remote(mine, mine, a_send.at[d], a_recv.at[d], (at(chip, d) * 2 + other, t))
        gather[d].start()
        if d == 7:
            far = remote(mine, mine, f_send.at[d], f_recv.at[d], (at(chip, d) * 2 + core, t))
            far.start()
    swap = remote(mine, mine, f_send.at[0], f_recv.at[0], sibling)
    swap.start()

    gain_load.wait()
    win_load.wait()
    gain_col = jnp.broadcast_to(gain[...], (128, COLS)).T
    for j in range(DDEP // 128):
        cols = slice(j * 128, (j + 1) * 128)
        win[:, cols] = (win[:, cols].astype(F32) * gain_col).astype(BF16)
    look_to_sib.wait()
    look_out[...] = (look_own[...].astype(F32) + look_in_sib[...].astype(F32)).astype(BF16)

    across = [far]
    for d in near_first:
        gather[d].wait_recv()
        if d < 7:
            block = attn_all.at[back(chip, d), other]
            copy = remote(block, block, f_send.at[d], f_recv.at[d], sibling)
            copy.start()
            across.append(copy)
    swap.wait_recv()
    wo_load.wait()

    reduce_tp = [{}, {}]

    def reduce_start(half, parity):
        rows = attn_all[:, pl.ds(parity, 1)].reshape(CHIPS * ROWS, GROUP * HD)
        part[half] = dot(rows, wo[...]).astype(BF16).reshape(CHIPS, ROWS, COLS)
        for d in far_first:
            to = at(t, d)
            copy = remote(part.at[half, to], part_in.at[half, d], b_send.at[half, d], b_recv.at[half, d], (s, to))
            copy.start()
            reduce_tp[half][d] = copy

    reduce_start(0, other)
    for copy in across:
        copy.wait_recv()
    reduce_start(1, core)
    look_copies = []
    for d in far_first:
        to = at(chip, d)
        copy = remote(look_out.at[to], look_in.at[d], l_send.at[d], l_recv.at[d], (to * 2 + core, t))
        copy.start()
        look_copies.append(copy)
    x_load.wait()
    gather_tp = [[], []]

    def gather_start(half, parity):
        hidden = xres[pl.ds(pl.multiple_of(parity * ROWS, ROWS), ROWS)].astype(F32) + part[half, t].astype(F32)
        for d in near_first:
            reduce_tp[half][d].wait_recv()
            hidden = hidden + part_in[half, d].astype(F32)
        hid_all[t, parity] = hidden.astype(BF16)
        block = hid_all.at[t, parity]
        for d in far_first:
            copy = remote(block, block, h_send.at[half, d], h_recv.at[half, d], (s, at(t, d)))
            copy.start()
            gather_tp[half].append(copy)

    gather_start(0, other)
    gather_start(1, core)

    lane = lax.broadcasted_iota(jnp.int32, (CHIPS * ROWS, 128), 1)

    def project(parity):
        rows = hid_all[:, pl.ds(parity, 1)].reshape(CHIPS * ROWS, COLS)
        wide = rows.astype(F32)
        squares = jnp.sum(wide * wide, axis=1, keepdims=True)
        high = squares.astype(BF16).astype(F32)
        low = squares - high
        extra = jnp.where(lane == 2 * core, high, 0.0) + jnp.where(lane == 2 * core + 1, low, 0.0)
        return dot(rows, win[...]).reshape(CHIPS, ROWS, DDEP), extra.reshape(CHIPS, ROWS, 128)

    for copy in gather_tp[0]:
        copy.wait_recv()
    product, extra = project(other)
    c_sib[:, :, :DDEP] = product.astype(BF16)
    c_sib[:, :, DDEP:] = extra.astype(BF16)
    to_sib = remote(c_sib, c_in_sib, sib_send.at[1], sib_recv.at[1], sibling)
    to_sib.start()
    looked = look_out[chip].astype(F32)
    for d in range(1, CHIPS):
        look_copies[7 - d].wait_recv()
        looked = looked + look_in[d].astype(F32)
    for copy in gather_tp[1]:
        copy.wait_recv()
    to_sib.wait()
    product, extra = project(core)
    c_out[:, :, :DDEP] = (product + c_in_sib[:, :, :DDEP].astype(F32)).astype(BF16)
    c_out[:, :, DDEP:] = (extra + c_in_sib[:, :, DDEP:].astype(F32)).astype(BF16)
    reduce_sess = {}
    for d in far_first:
        to = at(chip, d)
        copy = remote(c_out.at[to], c_in.at[d], c_send.at[d], c_recv.at[d], (to * 2 + core, t))
        copy.start()
        reduce_sess[d] = copy
    summed = c_out[chip].astype(F32)
    for d in near_first:
        reduce_sess[d].wait_recv()
        summed = summed + c_in[d].astype(F32)
    squares = jnp.sum(summed[:, DDEP:], axis=1, keepdims=True)
    depth_in = summed[:, :DDEP] * lax.rsqrt(squares / D + EPS) + looked

    dgain_load.wait()
    mean_sq = jnp.mean(depth_in * depth_in, axis=1, keepdims=True)
    normed = (depth_in * lax.rsqrt(mean_sq + EPS) * dgain[...]).astype(BF16)
    dqkv_load.wait()
    for u in range(4):
        for p in range(3):
            first = p * DDEP + u * QUAD
            d_out[u, :, p * QUAD : (p + 1) * QUAD] = dot(normed, dqkv[:, first : first + QUAD]).astype(BF16)
    down = []
    for e in (2, 1, 3, 0):
        to = (col + e) % 4
        source = d_out.at[to, :, QUAD:]
        down.append(
            remote(source, d_in.at[t, :, QUAD:], d_send.at[4 + e], d_recv.at[4 + e], (s, 4 + to))
        )

    @pl.when(row == 0)
    def _():
        for copy in down:
            copy.start()

    heads_out = []
    for e in (2, 1, 3):
        to = (col + e) % 4
        copy = remote(d_out.at[to], d_in.at[t], d_send.at[e], d_recv.at[e], (s, row * 4 + to))
        copy.start()
        heads_out.append(copy)
    d_in[t] = d_out[col]
    for copy in heads_out:
        copy.wait_recv()

    head_r = lax.broadcasted_iota(jnp.int32, (QUAD, QUAD), 0) // DH
    head_c = lax.broadcasted_iota(jnp.int32, (QUAD, QUAD), 1) // DH
    same_head = jnp.where(head_r == head_c, 1.0, 0.0).astype(BF16)

    def attend(codebooks):
        count = codebooks[-1] + 1
        qs = [d_in[c, :, :QUAD].astype(F32) for c in codebooks]
        ks = [d_in[c, :, QUAD : 2 * QUAD].astype(F32) for c in range(count)]
        vs = [d_in[c, :, 2 * QUAD :].astype(F32) for c in range(count)]
        products = jnp.concatenate(
            [qs[i] * ks[j] for i, c in enumerate(codebooks) for j in range(c + 1)], axis=0
        )
        high = products.astype(BF16)
        low = (products - high.astype(F32)).astype(BF16)
        scores = (dot(high, same_head) + dot(low, same_head)) * DH ** (-0.5)
        start = 0
        for i, c in enumerate(codebooks):
            lines = [scores[(start + j) * ROWS : (start + j + 1) * ROWS] for j in range(c + 1)]
            start += c + 1
            top = lines[0]
            for line in lines[1:]:
                top = jnp.maximum(top, line)
            total = jnp.zeros((ROWS, QUAD), F32)
            context = jnp.zeros((ROWS, QUAD), F32)
            for j, line in enumerate(lines):
                weight = jnp.exp(line - top)
                total = total + weight
                context = context + weight * vs[j]
            e_out[i] = (context / total).astype(BF16)

    @pl.when(row == 0)
    def _():
        attend((0, 1, 2, 3))

    @pl.when(row == 1)
    def _():
        for copy in down:
            copy.wait_recv()
        attend((4, 5, 6, 7))

    heads_back = []
    for e in (2, 1, 3):
        to = (col + e) % 4
        copy = remote(e_out.at[to], e_in.at[col], e_send.at[e], e_recv.at[e], (s, row * 4 + to))
        copy.start()
        heads_back.append(copy)
    e_in[col] = e_out[col]
    dout_load.wait()
    for copy in heads_back:
        copy.wait_recv()
    context = jnp.concatenate([e_in[i] for i in range(4)], axis=1)
    out_ref[...] = (depth_in + dot(context, dout[...])).astype(BF16)

    sent = list(gather.values()) + across + [swap] + gather_tp[0] + gather_tp[1] + look_copies + heads_out + heads_back
    for copies in (reduce_tp[0], reduce_tp[1], reduce_sess):
        sent += list(copies.values())
    for copy in sent:
        copy.wait_send()

    @pl.when(row == 0)
    def _():
        for copy in down:
            copy.wait_send()


def shards(
    x_resid,
    qkv_new,
    kv_cache,
    cache_lens,
    wo_temporal,
    norm_gain,
    w_in,
    embed_rows,
    token_ids,
    depth_gain,
    depth_qkv,
    depth_out,
):
    args = (
        x_resid,
        qkv_new.reshape(ROWS, (GROUP + 2) * HD),
        kv_cache.reshape(ROWS, 2, FRAMES, HD),
        cache_lens,
        wo_temporal,
        norm_gain.reshape(1, COLS),
        w_in.reshape(COLS, DDEP),
        embed_rows.reshape(128, DDEP),
        token_ids.reshape(1, 256),
        depth_gain,
        depth_qkv.reshape(DDEP, 3 * DDEP),
        depth_out.reshape(DDEP, DDEP),
    )
    args = tuple(pltpu.with_memory_space_constraint(a, pltpu.HBM) for a in args)
    dma = pltpu.SemaphoreType.DMA
    vm = pltpu.VMEM
    out = pl.pallas_call(
        frame_kernel,
        name="frame",
        out_shape=jax.ShapeDtypeStruct((ROWS, DDEP), BF16),
        in_specs=[pl.BlockSpec(memory_space=pltpu.HBM)] * len(args),
        out_specs=pl.BlockSpec(memory_space=pltpu.VMEM),
        scratch_shapes=[
            vm((ROWS, FRAMES, HD), BF16),
            vm((ROWS, FRAMES, HD), BF16),
            vm((GROUP * HD, COLS), BF16),
            vm((COLS, DDEP), BF16),
            vm((128, DDEP), BF16),
            vm((DDEP, 3 * DDEP), BF16),
            vm((DDEP, DDEP), BF16),
            vm((32, COLS), BF16),
            vm((ROWS, (GROUP + 2) * HD), BF16),
            pltpu.SMEM((ROWS,), jnp.int32),
            vm((1, COLS), F32),
            vm((1, DDEP), F32),
            vm((1, 256), jnp.int32),
            dma((2, ROWS // STEP)),
            dma((11,)),
            vm((ROWS * GROUP, HD), F32),
            vm((ROWS * GROUP, HD), F32),
            vm((ROWS * GROUP, HD), F32),
            vm((ROWS * HD, HD), BF16),
            vm((FRAMES, HD), F32),
            vm((ROWS * GROUP, FRAMES), F32),
            vm((ROWS * GROUP, HD), F32),
            vm((CHIPS, 2, ROWS, GROUP * HD), BF16),
            vm((2, TP, ROWS, COLS), BF16),
            vm((2, TP, ROWS, COLS), BF16),
            vm((TP, 2, ROWS, COLS), BF16),
            vm((CHIPS, 2, ROWS, 128), BF16),
            vm((CHIPS, ROWS, DDEP), BF16),
            vm((CHIPS, ROWS, DDEP), BF16),
            vm((CHIPS, ROWS, DDEP), BF16),
            vm((CHIPS, ROWS, DDEP), BF16),
            vm((CHIPS, ROWS, DDEP), BF16),
            vm((CHIPS, ROWS, WIDE), BF16),
            vm((CHIPS, ROWS, WIDE), BF16),
            vm((CHIPS, ROWS, WIDE), BF16),
            vm((CHIPS, ROWS, WIDE), BF16),
            vm((4, ROWS, 3 * QUAD), BF16),
            vm((TP, ROWS, 3 * QUAD), BF16),
            vm((4, ROWS, QUAD), BF16),
            vm((4, ROWS, QUAD), BF16),
            dma((8,)),
            dma((8,)),
            dma((8,)),
            dma((8,)),
            dma((2, 8)),
            dma((2, 8)),
            dma((2, 8)),
            dma((2, 8)),
            dma((8,)),
            dma((8,)),
            dma((8,)),
            dma((8,)),
            dma((4,)),
            dma((4,)),
            dma((8,)),
            dma((8,)),
            dma((2,)),
            dma((2,)),
        ],
        compiler_params=pltpu.CompilerParams(
            collective_id=0, has_side_effects=True, vmem_limit_bytes=62 * 2**20
        ),
        cost_estimate=pl.CostEstimate(flops=10**9, bytes_accessed=19 * 10**6, transcendentals=10**5),
    )(*args)
    return out.reshape(ROWS, 1, DDEP)


def solution(mesh):
    in_specs = (
        P(None, "sess"),
        P("sess", "tp", None),
        P("sess", None, "tp", None, None),
        P("sess"),
        P("tp", "sess"),
        P("sess"),
        P("tp", "sess", None),
        P("tp", "sess", None),
        P(None, "tp"),
        P("tp", None),
        P("tp", None, None),
        P("tp", None, None),
    )
    out_specs = P("sess", "tp", None)
    return jax.shard_map(shards, mesh=mesh, in_specs=in_specs, out_specs=out_specs, check_vma=False)
```

```python
import jax
import jax.numpy as jnp
from jax import lax
from jax.experimental import pallas as pl
from jax.experimental.pallas import tpu as pltpu
from jax.sharding import PartitionSpec as P

MESH = pl.DeviceIdType.MESH
F32 = jnp.float32
BF16 = jnp.bfloat16

D = 8192
EPS = 1e-05
CHIPS = 8
TP = 8
ROWS = 16
GROUP = 8
HD = 128
FRAMES = 1024
COLS = 512
DDEP = 1024
WIDE = DDEP + 128
QUAD = 256
DH = 64
STEP = 4


def dot(a, b):
    return jnp.dot(a, b, preferred_element_type=F32)


def frame_kernel(
    x_hbm,
    qkv_hbm,
    kv_hbm,
    lens_hbm,
    wo_hbm,
    gain_hbm,
    win_hbm,
    emb_hbm,
    tok_hbm,
    dgain_hbm,
    dqkv_hbm,
    dout_hbm,
    out_ref,
    keys,
    values,
    wo,
    win,
    emb,
    dqkv,
    dout,
    xres,
    qkv,
    lens,
    gain,
    dgain,
    tok,
    kv_sem,
    in_sem,
    q_scr,
    k_scr,
    v_scr,
    query_cols,
    score_scr,
    weight_scr,
    o_scr,
    attn_all,
    part,
    part_in,
    hid_all,
    onehot,
    look_own,
    look_sib,
    look_in_sib,
    look_out,
    look_in,
    c_sib,
    c_in_sib,
    c_out,
    c_in,
    d_out,
    d_in,
    e_out,
    e_in,
    direct_sem,
    sems,
):
    s = lax.axis_index("sess")
    t = lax.axis_index("tp")
    chip = s // 2
    core = s % 2
    other = 1 - core
    row = t // 4
    col = t % 4
    sibling = (chip * 2 + other, t)

    def step_of(d):
        return ((0, 0), (0, 1), (0, 3), (1, 0), (0, 2), (1, 1), (1, 3), (1, 2))[d]

    def at(i, d):
        hi, lo = step_of(d)
        return ((i // 4 + hi) % 2) * 4 + (i % 4 + lo) % 4

    def back(i, d):
        hi, lo = step_of(d)
        return ((i // 4 + hi) % 2) * 4 + (i % 4 + 4 - lo) % 4

    far_first = (7, 6, 5, 4, 3, 2, 1)
    near_first = (1, 2, 3, 4, 5, 6, 7)

    def remote(src, dst, send, recv, device):
        return pltpu.make_async_remote_copy(
            src_ref=src,
            dst_ref=dst,
            send_sem=send,
            recv_sem=recv,
            device_id=device,
            device_id_type=MESH,
        )

    def settle(ref, sem):
        pltpu.make_async_copy(ref, ref, sem).wait()

    def load(i, src, dst):
        return pltpu.make_async_copy(src, dst, in_sem.at[i])

    x_load = load(0, x_hbm.at[pl.ds(pl.multiple_of(t * 32, 32), 32)], xres)
    qkv_load = load(1, qkv_hbm, qkv)
    lens_load = load(2, lens_hbm, lens)
    gain_load = load(3, gain_hbm, gain)
    dgain_load = load(4, dgain_hbm, dgain)
    tok_load = load(5, tok_hbm, tok)
    emb_load = load(6, emb_hbm, emb)
    wo_load = load(7, wo_hbm, wo)
    win_load = load(8, win_hbm, win)
    dqkv_load = load(9, dqkv_hbm, dqkv)
    dout_load = load(10, dout_hbm, dout)
    key_loads = [
        pltpu.make_async_copy(kv_hbm.at[pl.ds(g * STEP, STEP), 0], keys.at[pl.ds(g * STEP, STEP)], kv_sem.at[0, g])
        for g in range(ROWS // STEP)
    ]
    value_loads = [
        pltpu.make_async_copy(kv_hbm.at[pl.ds(g * STEP, STEP), 1], values.at[pl.ds(g * STEP, STEP)], kv_sem.at[1, g])
        for g in range(ROWS // STEP)
    ]
    for copy in [qkv_load, lens_load, tok_load, emb_load] + key_loads + value_loads:
        copy.start()
    for copy in (gain_load, dgain_load, x_load):
        copy.start()

    barrier = pltpu.get_barrier_semaphore()
    pl.semaphore_signal(barrier, inc=1, device_id=sibling, device_id_type=MESH)
    for d in near_first:
        for device in ((at(chip, d) * 2, t), (at(chip, d) * 2 + 1, t), (s, at(t, d))):
            pl.semaphore_signal(barrier, inc=1, device_id=device, device_id_type=MESH)

    qkv_load.wait()
    new_keys = qkv[:, GROUP * HD : (GROUP + 1) * HD].astype(F32)
    new_values = qkv[:, (GROUP + 1) * HD :].astype(F32)
    for h in range(GROUP):
        rows_h = pl.ds(h, ROWS, stride=GROUP)
        q_scr[rows_h, :] = qkv[:, h * HD : (h + 1) * HD].astype(F32)
        k_scr[rows_h, :] = new_keys
        v_scr[rows_h, :] = new_values
    query_t = q_scr[...].T
    scale = HD ** (-0.5)
    new_score = jnp.sum(query_t * k_scr[...].T, axis=0, keepdims=True) * scale
    owner = lax.broadcasted_iota(jnp.int32, (HD, HD), 1) // GROUP
    for i in range(ROWS):
        query_cols[i * HD : (i + 1) * HD, :] = jnp.where(owner == i, query_t, 0.0).astype(BF16)
    lens_load.wait()
    owner_row = lax.broadcasted_iota(jnp.int32, (1, HD), 1) // GROUP
    live = jnp.zeros((1, HD), jnp.int32)
    for i in range(ROWS):
        live = jnp.where(owner_row == i, lens[i], live)

    tok_load.wait()
    emb_load.wait()
    entry = lax.broadcasted_iota(jnp.int32, (128, 256), 0) + s * 128
    hot = jnp.where(tok[...] == entry, 1.0, 0.0).T.astype(BF16)
    onehot[...] = hot.reshape(CHIPS, 2, ROWS, 128)

    def look(parity):
        rows = onehot[:, pl.ds(parity, 1)].reshape(CHIPS * ROWS, 128)
        return dot(rows, emb[...]).astype(BF16).reshape(CHIPS, ROWS, DDEP)

    look_sib[...] = look(other)
    look_own[...] = look(core)

    for g in range(ROWS // STEP):
        key_loads[g].wait()
        joined = jnp.concatenate([keys[g * STEP + i] for i in range(STEP)], axis=1)
        scores = dot(joined, query_cols[g * STEP * HD : (g + 1) * STEP * HD, :])
        if g == 0:
            score_scr[...] = scores
        else:
            score_scr[...] += scores
    wo_load.start()
    win_load.start()
    pl.semaphore_wait(barrier, 22)
    look_to_sib = remote(look_sib, look_in_sib, sems.at[0], sems.at[1], sibling)
    look_to_sib.start()

    frame = lax.broadcasted_iota(jnp.int32, (FRAMES, HD), 0)
    masked = jnp.where(frame < live, score_scr[...] * scale, -1e30)
    peak = jnp.maximum(jnp.max(masked, axis=0, keepdims=True), new_score)
    expo = jnp.exp(masked - peak)
    new_expo = jnp.exp(new_score - peak)
    inv = 1.0 / (jnp.sum(expo, axis=0, keepdims=True) + new_expo)
    weight_scr[...] = (expo * inv).T
    new_weight = (new_expo * inv).astype(BF16).astype(F32)
    o_scr[...] = jnp.broadcast_to(new_weight, (HD, HD)).T * v_scr[...]
    for g in range(ROWS // STEP):
        value_loads[g].wait()
        for i in range(g * STEP, (g + 1) * STEP):
            rows_i = slice(i * GROUP, (i + 1) * GROUP)
            o_scr[rows_i, :] += dot(weight_scr[rows_i, :].astype(BF16), values[i])
    dqkv_load.start()
    dout_load.start()

    for h in range(GROUP):
        attn_all[chip, core, :, h * HD : (h + 1) * HD] = o_scr[pl.ds(h, ROWS, stride=GROUP), :].astype(BF16)
    mine = attn_all.at[chip, core]
    gather = {}
    for d in far_first:
        gather[d] = remote(mine, mine, sems.at[2], direct_sem.at[d - 1], (at(chip, d) * 2 + other, t))
        gather[d].start()
        if d == 7:
            remote(mine, mine, sems.at[3], sems.at[4], (at(chip, d) * 2 + core, t)).start()
    swap = remote(mine, mine, sems.at[5], sems.at[6], sibling)
    swap.start()

    gain_load.wait()
    win_load.wait()
    gain_col = jnp.broadcast_to(gain[...], (128, COLS)).T
    for j in range(DDEP // 128):
        cols = slice(j * 128, (j + 1) * 128)
        win[:, cols] = (win[:, cols].astype(F32) * gain_col).astype(BF16)
    look_to_sib.wait_recv()
    look_out[...] = (look_own[...].astype(F32) + look_in_sib[...].astype(F32)).astype(BF16)

    for d in near_first:
        gather[d].wait_recv()
        if d < 7:
            block = attn_all.at[back(chip, d), other]
            remote(block, block, sems.at[3], sems.at[4], sibling).start()
    swap.wait_recv()
    wo_load.wait()

    def reduce_start(half, parity):
        rows = attn_all[:, pl.ds(parity, 1)].reshape(CHIPS * ROWS, GROUP * HD)
        part[half] = dot(rows, wo[...]).astype(BF16).reshape(CHIPS, ROWS, COLS)
        for d in far_first:
            to = at(t, d)
            remote(part.at[half, to], part_in.at[half, d - 1], sems.at[7 + half], sems.at[9 + half], (s, to)).start()

    reduce_start(0, other)
    settle(look_in, sems.at[4])
    reduce_start(1, core)
    for d in far_first:
        to = at(chip, d)
        remote(look_out.at[to], look_in.at[d - 1], sems.at[15], sems.at[16], (to * 2 + core, t)).start()
    x_load.wait()

    def gather_start(half, parity):
        hidden = xres[pl.ds(pl.multiple_of(parity * ROWS, ROWS), ROWS)].astype(F32) + part[half, t].astype(F32)
        settle(part_in.at[half], sems.at[9 + half])
        for d in range(CHIPS - 1):
            hidden = hidden + part_in[half, d].astype(F32)
        hid_all[t, parity] = hidden.astype(BF16)
        block = hid_all.at[t, parity]
        for d in far_first:
            remote(block, block, sems.at[11 + half], sems.at[13 + half], (s, at(t, d))).start()

    gather_start(0, other)
    gather_start(1, core)

    lane = lax.broadcasted_iota(jnp.int32, (4 * ROWS, 128), 1)

    def project(parity, blocks):
        rows = jnp.concatenate([hid_all[i, parity] for i in blocks], axis=0)
        wide = rows.astype(F32)
        squares = jnp.sum(wide * wide, axis=1, keepdims=True)
        high = squares.astype(BF16).astype(F32)
        low = squares - high
        extra = jnp.where(lane == 2 * core, high, 0.0) + jnp.where(lane == 2 * core + 1, low, 0.0)
        return dot(rows, win[...]).reshape(len(blocks), ROWS, DDEP), extra.reshape(len(blocks), ROWS, 128)

    settle(part_in.at[0], sems.at[13])
    for blocks in (range(4), range(4, 8)):
        product, extra = project(other, blocks)
        c_sib[blocks[0] : blocks[0] + 4, :, :DDEP] = product.astype(BF16)
        c_sib[blocks[0] : blocks[0] + 4, :, DDEP:] = extra.astype(BF16)
    to_sib = remote(c_sib, c_in_sib, sems.at[17], sems.at[18], sibling)
    to_sib.start()
    settle(look_in, sems.at[16])
    looked = look_out[chip].astype(F32)
    for d in range(CHIPS - 1):
        looked = looked + look_in[d].astype(F32)
    settle(part_in.at[1], sems.at[14])
    to_sib.wait_recv()
    for offsets in ((7, 6, 5, 4), (3, 2, 1, 0)):
        product, extra = project(core, [at(chip, d) for d in offsets])
        for i, d in enumerate(offsets):
            to = at(chip, d)
            c_out[d, :, :DDEP] = (product[i] + c_in_sib[to, :, :DDEP].astype(F32)).astype(BF16)
            c_out[d, :, DDEP:] = (extra[i] + c_in_sib[to, :, DDEP:].astype(F32)).astype(BF16)
            if d:
                remote(c_out.at[d], c_in.at[d - 1], sems.at[19], sems.at[20], (to * 2 + core, t)).start()
    summed = c_out[0].astype(F32)
    settle(c_in, sems.at[20])
    for d in range(CHIPS - 1):
        summed = summed + c_in[d].astype(F32)
    squares = jnp.sum(summed[:, DDEP:], axis=1, keepdims=True)
    depth_in = summed[:, :DDEP] * lax.rsqrt(squares / D + EPS) + looked

    dgain_load.wait()
    mean_sq = jnp.mean(depth_in * depth_in, axis=1, keepdims=True)
    normed = (depth_in * lax.rsqrt(mean_sq + EPS) * dgain[...]).astype(BF16)
    dqkv_load.wait()
    for e in (2, 1, 3, 0):
        to = (col + e) % 4
        for p in range(3):
            first = pl.multiple_of(p * DDEP + to * QUAD, QUAD)
            d_out[e, :, p * QUAD : (p + 1) * QUAD] = dot(normed, dqkv[:, pl.ds(first, QUAD)]).astype(BF16)

        @pl.when(row == 0)
        def _(e=e, to=to):
            remote(
                d_out.at[e, :, QUAD:], d_in.at[t, :, QUAD:], sems.at[21], sems.at[22], (s, 4 + to)
            ).start()

        if e:
            remote(d_out.at[e], d_in.at[t], sems.at[23], sems.at[24], (s, row * 4 + to)).start()
    d_in[t] = d_out[0]
    settle(d_in.at[pl.ds(0, 3)], sems.at[24])

    head_r = lax.broadcasted_iota(jnp.int32, (QUAD, QUAD), 0) // DH
    head_c = lax.broadcasted_iota(jnp.int32, (QUAD, QUAD), 1) // DH
    same_head = jnp.where(head_r == head_c, 1.0, 0.0).astype(BF16)

    def attend(codebooks):
        count = codebooks[-1] + 1
        qs = [d_in[c, :, :QUAD].astype(F32) for c in codebooks]
        ks = [d_in[c, :, QUAD : 2 * QUAD].astype(F32) for c in range(count)]
        vs = [d_in[c, :, 2 * QUAD :].astype(F32) for c in range(count)]
        products = jnp.concatenate(
            [qs[i] * ks[j] for i, c in enumerate(codebooks) for j in range(c + 1)], axis=0
        )
        high = products.astype(BF16)
        low = (products - high.astype(F32)).astype(BF16)
        scores = (dot(high, same_head) + dot(low, same_head)) * DH ** (-0.5)
        start = 0
        for i, c in enumerate(codebooks):
            lines = [scores[(start + j) * ROWS : (start + j + 1) * ROWS] for j in range(c + 1)]
            start += c + 1
            top = lines[0]
            for line in lines[1:]:
                top = jnp.maximum(top, line)
            total = jnp.zeros((ROWS, QUAD), F32)
            context = jnp.zeros((ROWS, QUAD), F32)
            for j, line in enumerate(lines):
                weight = jnp.exp(line - top)
                total = total + weight
                context = context + weight * vs[j]
            e_out[i] = (context / total).astype(BF16)

    @pl.when(row == 0)
    def _():
        attend((0, 1, 2, 3))

    @pl.when(row == 1)
    def _():
        settle(d_in.at[pl.ds(0, 4), :, QUAD:], sems.at[22])
        attend((4, 5, 6, 7))

    for e in (2, 1, 3):
        to = (col + e) % 4
        remote(e_out.at[to], e_in.at[col], sems.at[25], sems.at[26], (s, row * 4 + to)).start()
    e_in[col] = e_out[col]
    dout_load.wait()
    settle(e_in.at[pl.ds(0, 3)], sems.at[26])
    context = jnp.concatenate([e_in[i] for i in range(4)], axis=1)
    out_ref[...] = (depth_in + dot(context, dout[...])).astype(BF16)

    for ref, i in (
        (look_sib, 0),
        (look_in, 2),
        (look_in, 3),
        (mine, 5),
        (part_in.at[0], 7),
        (part_in.at[1], 8),
        (part_in.at[0], 11),
        (part_in.at[1], 12),
        (look_in, 15),
        (c_sib, 17),
        (c_in, 19),
        (d_in.at[pl.ds(0, 3)], 23),
        (e_in.at[pl.ds(0, 3)], 25),
    ):
        settle(ref, sems.at[i])

    @pl.when(row == 0)
    def _():
        settle(d_in.at[pl.ds(0, 4), :, QUAD:], sems.at[21])


def shards(
    x_resid,
    qkv_new,
    kv_cache,
    cache_lens,
    wo_temporal,
    norm_gain,
    w_in,
    embed_rows,
    token_ids,
    depth_gain,
    depth_qkv,
    depth_out,
):
    args = (
        x_resid,
        qkv_new.reshape(ROWS, (GROUP + 2) * HD),
        kv_cache.reshape(ROWS, 2, FRAMES, HD),
        cache_lens,
        wo_temporal,
        norm_gain.reshape(1, COLS),
        w_in.reshape(COLS, DDEP),
        embed_rows.reshape(128, DDEP),
        token_ids.reshape(1, 256),
        depth_gain,
        depth_qkv.reshape(DDEP, 3 * DDEP),
        depth_out.reshape(DDEP, DDEP),
    )
    args = tuple(pltpu.with_memory_space_constraint(a, pltpu.HBM) for a in args)
    dma = pltpu.SemaphoreType.DMA
    vm = pltpu.VMEM
    out = pl.pallas_call(
        frame_kernel,
        name="frame",
        out_shape=jax.ShapeDtypeStruct((ROWS, DDEP), BF16),
        in_specs=[pl.BlockSpec(memory_space=pltpu.HBM)] * len(args),
        out_specs=pl.BlockSpec(memory_space=pltpu.VMEM),
        scratch_shapes=[
            vm((ROWS, FRAMES, HD), BF16),
            vm((ROWS, FRAMES, HD), BF16),
            vm((GROUP * HD, COLS), BF16),
            vm((COLS, DDEP), BF16),
            vm((128, DDEP), BF16),
            vm((DDEP, 3 * DDEP), BF16),
            vm((DDEP, DDEP), BF16),
            vm((32, COLS), BF16),
            vm((ROWS, (GROUP + 2) * HD), BF16),
            pltpu.SMEM((ROWS,), jnp.int32),
            vm((1, COLS), F32),
            vm((1, DDEP), F32),
            vm((1, 256), jnp.int32),
            dma((2, ROWS // STEP)),
            dma((11,)),
            vm((ROWS * GROUP, HD), F32),
            vm((ROWS * GROUP, HD), F32),
            vm((ROWS * GROUP, HD), F32),
            vm((ROWS * HD, HD), BF16),
            vm((FRAMES, HD), F32),
            vm((ROWS * GROUP, FRAMES), F32),
            vm((ROWS * GROUP, HD), F32),
            vm((CHIPS, 2, ROWS, GROUP * HD), BF16),
            vm((2, TP, ROWS, COLS), BF16),
            vm((2, TP - 1, ROWS, COLS), BF16),
            vm((TP, 2, ROWS, COLS), BF16),
            vm((CHIPS, 2, ROWS, 128), BF16),
            vm((CHIPS, ROWS, DDEP), BF16),
            vm((CHIPS, ROWS, DDEP), BF16),
            vm((CHIPS, ROWS, DDEP), BF16),
            vm((CHIPS, ROWS, DDEP), BF16),
            vm((CHIPS - 1, ROWS, DDEP), BF16),
            vm((CHIPS, ROWS, WIDE), BF16),
            vm((CHIPS, ROWS, WIDE), BF16),
            vm((CHIPS, ROWS, WIDE), BF16),
            vm((CHIPS - 1, ROWS, WIDE), BF16),
            vm((4, ROWS, 3 * QUAD), BF16),
            vm((TP, ROWS, 3 * QUAD), BF16),
            vm((4, ROWS, QUAD), BF16),
            vm((4, ROWS, QUAD), BF16),
            dma((7,)),
            dma((27,)),
        ],
        compiler_params=pltpu.CompilerParams(
            collective_id=0, has_side_effects=True, vmem_limit_bytes=40 * 2**20
        ),
        cost_estimate=pl.CostEstimate(flops=10**9, bytes_accessed=19 * 10**6, transcendentals=10**5),
    )(*args)
    return out.reshape(ROWS, 1, DDEP)


def solution(mesh):
    in_specs = (
        P(None, "sess"),
        P("sess", "tp", None),
        P("sess", None, "tp", None, None),
        P("sess"),
        P("tp", "sess"),
        P("sess"),
        P("tp", "sess", None),
        P("tp", "sess", None),
        P(None, "tp"),
        P("tp", None),
        P("tp", None, None),
        P("tp", None, None),
    )
    out_specs = P("sess", "tp", None)
    return jax.shard_map(shards, mesh=mesh, in_specs=in_specs, out_specs=out_specs, check_vma=False)
```

```python
import jax
import jax.numpy as jnp
from jax import lax
from jax.experimental import pallas as pl
from jax.experimental.pallas import tpu as pltpu
from jax.sharding import PartitionSpec as P

MESH = pl.DeviceIdType.MESH
F32 = jnp.float32
BF16 = jnp.bfloat16

D = 8192
EPS = 1e-05
CHIPS = 8
TP = 8
ROWS = 16
GROUP = 8
HD = 128
FRAMES = 1024
COLS = 512
DDEP = 1024
WIDE = DDEP + 128
QUAD = 256
DH = 64
HALF = 8
HALF_FRAMES = FRAMES // 2


def dot(a, b):
    return jnp.dot(a, b, preferred_element_type=F32)


def frame_kernel(
    x_hbm,
    qkv_hbm,
    kv_hbm,
    lens_hbm,
    wo_hbm,
    gain_hbm,
    win_hbm,
    emb_hbm,
    tok_hbm,
    dgain_hbm,
    dqkv_hbm,
    dout_hbm,
    out_ref,
    keys,
    values,
    wo,
    win,
    emb,
    dqkv,
    dout,
    xres,
    qkv,
    lens,
    gain,
    dgain,
    tok,
    kv_sem,
    in_sem,
    q_scr,
    k_scr,
    v_scr,
    query_cols,
    weight_scr,
    o_scr,
    attn_all,
    part,
    part_in,
    hid_all,
    onehot,
    look_own,
    look_sib,
    look_in_sib,
    look_out,
    look_in,
    c_sib,
    c_in_sib,
    c_out,
    c_in,
    d_out,
    d_in,
    e_out,
    e_in,
    direct_sem,
    sems,
):
    s = lax.axis_index("sess")
    t = lax.axis_index("tp")
    chip = s // 2
    core = s % 2
    other = 1 - core
    row = t // 4
    col = t % 4
    sibling = (chip * 2 + other, t)

    def step_of(d):
        return ((0, 0), (0, 1), (0, 3), (1, 0), (0, 2), (1, 1), (1, 3), (1, 2))[d]

    def at(i, d):
        hi, lo = step_of(d)
        return ((i // 4 + hi) % 2) * 4 + (i % 4 + lo) % 4

    def back(i, d):
        hi, lo = step_of(d)
        return ((i // 4 + hi) % 2) * 4 + (i % 4 + 4 - lo) % 4

    far_first = (7, 6, 5, 4, 3, 2, 1)
    near_first = (1, 2, 3, 4, 5, 6, 7)

    def remote(src, dst, send, recv, device):
        return pltpu.make_async_remote_copy(
            src_ref=src,
            dst_ref=dst,
            send_sem=send,
            recv_sem=recv,
            device_id=device,
            device_id_type=MESH,
        )

    def settle(ref, sem):
        pltpu.make_async_copy(ref, ref, sem).wait()

    def load(i, src, dst):
        return pltpu.make_async_copy(src, dst, in_sem.at[i])

    x_load = load(0, x_hbm.at[pl.ds(pl.multiple_of(t * 32, 32), 32)], xres)
    qkv_load = load(1, qkv_hbm, qkv)
    lens_load = load(2, lens_hbm, lens)
    gain_load = load(3, gain_hbm, gain)
    dgain_load = load(4, dgain_hbm, dgain)
    tok_load = load(5, tok_hbm, tok)
    emb_load = load(6, emb_hbm, emb)
    wo_load = load(7, wo_hbm, wo)
    win_load = load(8, win_hbm, win)
    dqkv_load = load(9, dqkv_hbm, dqkv)
    dout_load = load(10, dout_hbm, dout)
    def cache_load(which, first, count, dst, i):
        part_of = pl.ds(first, count)
        return pltpu.make_async_copy(kv_hbm.at[part_of, which], dst.at[part_of], kv_sem.at[i])

    key_loads = [cache_load(0, a * HALF, HALF, keys, a) for a in range(2)]
    value_loads = [cache_load(1, g * 4, 4, values, 2 + g) for g in range(4)]
    loads = [qkv_load, key_loads[0], lens_load, value_loads[0], value_loads[1], key_loads[1], value_loads[2], value_loads[3]]
    for copy in loads:
        copy.start()

    barrier = pltpu.get_barrier_semaphore()
    pl.semaphore_signal(barrier, inc=1, device_id=sibling, device_id_type=MESH)
    for d in far_first:
        for device in ((at(chip, d) * 2, t), (at(chip, d) * 2 + 1, t), (s, at(t, d))):
            pl.semaphore_signal(barrier, inc=1, device_id=device, device_id_type=MESH)
    for copy in (tok_load, emb_load, gain_load, dgain_load, x_load):
        copy.start()

    qkv_load.wait()
    new_keys = qkv[:, GROUP * HD : (GROUP + 1) * HD].astype(F32)
    new_values = qkv[:, (GROUP + 1) * HD :].astype(F32)
    for h in range(GROUP):
        rows_h = pl.ds(h, ROWS, stride=GROUP)
        q_scr[rows_h, :] = qkv[:, h * HD : (h + 1) * HD].astype(F32)
        k_scr[rows_h, :] = new_keys
        v_scr[rows_h, :] = new_values
    query_t = q_scr[...].T
    scale = HD ** (-0.5)
    new_score = jnp.sum(query_t * k_scr[...].T, axis=0, keepdims=True) * scale
    new_score = jnp.broadcast_to(new_score, (8, HD))
    column = lax.broadcasted_iota(jnp.int32, (HD, HD), 1)
    line = lax.broadcasted_iota(jnp.int32, (8, HD), 1)
    swapped = pltpu.roll(query_t, 64, 1)
    swapped_score = pltpu.roll(new_score, 64, 1)
    lens_load.wait()
    half_scores = []
    lives = []
    for a in range(2):
        half_query = jnp.where((column < 64) == (a == 0), query_t, swapped)
        half_scores.append(jnp.where((line < 64) == (a == 0), new_score, swapped_score))
        live = jnp.zeros((8, HD), jnp.int32)
        for i in range(HALF):
            live = jnp.where((line // GROUP) % HALF == i, lens[a * HALF + i], live)
            for f in range(2):
                block = f * HALF + i
                query_cols[a, block * HD : (block + 1) * HD, :] = jnp.where(
                    column // GROUP == block, half_query, 0.0
                ).astype(BF16)
        lives.append(live - jnp.where(line < 64, 0, HALF_FRAMES))
    frame = lax.broadcasted_iota(jnp.int32, (HALF_FRAMES, HD), 0)

    def attend_half(a):
        key_loads[a].wait()
        joined = jnp.concatenate(
            [
                keys[a * HALF + i, f * HALF_FRAMES : (f + 1) * HALF_FRAMES]
                for f in range(2)
                for i in range(HALF)
            ],
            axis=1,
        )
        scores = dot(joined, query_cols[a]) * scale
        masked = jnp.where(frame < lives[a][:1], scores, -1e30)
        top = jnp.broadcast_to(jnp.max(masked, axis=0, keepdims=True), (8, HD))
        peak = jnp.maximum(jnp.maximum(top, pltpu.roll(top, 64, 1)), half_scores[a])
        expo = jnp.exp(masked - peak[:1])
        new_expo = jnp.exp(half_scores[a] - peak)
        total = jnp.broadcast_to(jnp.sum(expo, axis=0, keepdims=True), (8, HD))
        inv = 1.0 / (total + pltpu.roll(total, 64, 1) + new_expo)
        weight_scr[...] = (expo * inv[:1]).T
        new_weight = (new_expo * inv).astype(BF16).astype(F32)
        new_column = jnp.broadcast_to(new_weight[:1], (HD, HD)).T
        for g in range(2):
            value_loads[a * 2 + g].wait()
            for i in range(g * 4, g * 4 + 4):
                session = a * HALF + i
                rows_i = slice(i * GROUP, (i + 1) * GROUP)
                rows_s = slice(session * GROUP, (session + 1) * GROUP)
                context = new_column[rows_i] * v_scr[rows_s, :]
                for f in range(2):
                    weights = weight_scr[f * 64 + i * GROUP : f * 64 + (i + 1) * GROUP, :].astype(BF16)
                    context = context + dot(weights, values[session, f * HALF_FRAMES : (f + 1) * HALF_FRAMES])
                o_scr[rows_s, :] = context

    gather = {}

    def gather_half(a):
        for h in range(4):
            low_heads = o_scr[pl.ds(a * 64 + h, HALF, stride=GROUP), :]
            high_heads = o_scr[pl.ds(a * 64 + h + 4, HALF, stride=GROUP), :]
            attn_all[a, chip, core, :, h * HD : (h + 1) * HD] = jnp.concatenate(
                [low_heads, high_heads], axis=0
            ).astype(BF16)
        mine = attn_all.at[a, chip, core]
        if a == 0:
            pl.semaphore_wait(barrier, 22)
        for d in far_first:
            gather[a, d] = remote(
                mine, mine, sems.at[2], direct_sem.at[a * 7 + d - 1], (at(chip, d) * 2 + other, t)
            )
            gather[a, d].start()
            if d == 7:
                remote(mine, mine, sems.at[3], sems.at[4], (at(chip, d) * 2 + core, t)).start()
        remote(mine, mine, sems.at[5], sems.at[6], sibling).start()

    attend_half(0)
    gather_half(0)
    wo_load.start()
    win_load.start()
    attend_half(1)
    gather_half(1)
    dqkv_load.start()
    dout_load.start()

    tok_load.wait()
    emb_load.wait()
    entry = lax.broadcasted_iota(jnp.int32, (128, 256), 0) + s * 128
    hot = jnp.where(tok[...] == entry, 1.0, 0.0).T.astype(BF16)
    onehot[...] = hot.reshape(CHIPS, 2, ROWS, 128)

    def look(parity):
        rows = onehot[:, pl.ds(parity, 1)].reshape(CHIPS * ROWS, 128)
        return dot(rows, emb[...]).astype(BF16).reshape(CHIPS, ROWS, DDEP)

    look_sib[...] = look(other)
    look_to_sib = remote(look_sib, look_in_sib, sems.at[0], sems.at[1], sibling)
    look_to_sib.start()
    look_own[...] = look(core)

    gain_load.wait()
    win_load.wait()
    gain_col = jnp.broadcast_to(gain[...], (128, COLS)).T
    for j in range(DDEP // 128):
        cols = slice(j * 128, (j + 1) * 128)
        win[:, cols] = (win[:, cols].astype(F32) * gain_col).astype(BF16)

    for a in range(2):
        for d in near_first:
            gather[a, d].wait_recv()
            if d < 7:
                block = attn_all.at[a, back(chip, d), other]
                remote(block, block, sems.at[3], sems.at[4], sibling).start()
    settle(look_in.at[0], sems.at[6])
    wo_load.wait()

    def attention_rows(parity):
        blocks = []
        for i in range(CHIPS):
            for a in range(2):
                block = attn_all[a, i, parity].astype(F32)
                blocks.append(jnp.concatenate([block[:HALF], block[HALF:]], axis=1))
        return jnp.concatenate(blocks, axis=0).astype(BF16)

    def reduce_start(half, parity):
        part[half] = dot(attention_rows(parity), wo[...]).astype(BF16).reshape(CHIPS, ROWS, COLS)
        for d in far_first:
            to = at(t, d)
            remote(part.at[half, to], part_in.at[half, d - 1], sems.at[7 + half], sems.at[9 + half], (s, to)).start()

    reduce_start(0, other)
    settle(look_in, sems.at[4])
    reduce_start(1, core)
    look_to_sib.wait_recv()
    look_out[...] = (look_own[...].astype(F32) + look_in_sib[...].astype(F32)).astype(BF16)
    for d in far_first:
        to = at(chip, d)
        remote(look_out.at[to], look_in.at[d - 1], sems.at[15], sems.at[16], (to * 2 + core, t)).start()
    x_load.wait()

    def gather_start(half, parity):
        hidden = xres[pl.ds(pl.multiple_of(parity * ROWS, ROWS), ROWS)].astype(F32) + part[half, t].astype(F32)
        settle(part_in.at[half], sems.at[9 + half])
        for d in range(CHIPS - 1):
            hidden = hidden + part_in[half, d].astype(F32)
        hid_all[t, parity] = hidden.astype(BF16)
        block = hid_all.at[t, parity]
        for d in far_first:
            remote(block, block, sems.at[11 + half], sems.at[13 + half], (s, at(t, d))).start()

    gather_start(0, other)
    gather_start(1, core)

    lane = lax.broadcasted_iota(jnp.int32, (4 * ROWS, 128), 1)

    def project(parity, blocks):
        rows = jnp.concatenate([hid_all[i, parity] for i in blocks], axis=0)
        wide = rows.astype(F32)
        squares = jnp.sum(wide * wide, axis=1, keepdims=True)
        high = squares.astype(BF16).astype(F32)
        low = squares - high
        extra = jnp.where(lane == 2 * core, high, 0.0) + jnp.where(lane == 2 * core + 1, low, 0.0)
        return dot(rows, win[...]).reshape(len(blocks), ROWS, DDEP), extra.reshape(len(blocks), ROWS, 128)

    settle(part_in.at[0], sems.at[13])
    to_sib = {}
    for k, offsets in enumerate(((7, 6, 5, 4), (3, 2, 1, 0))):
        product, extra = project(other, [at(chip, d) for d in offsets])
        for i, d in enumerate(offsets):
            c_sib[d, :, :DDEP] = product[i].astype(BF16)
            c_sib[d, :, DDEP:] = extra[i].astype(BF16)
        part_of = pl.ds(offsets[3], 4)
        to_sib[k] = remote(
            c_sib.at[part_of], c_in_sib.at[part_of], sems.at[17], sems.at[18 if k == 0 else 27], sibling
        )
        to_sib[k].start()
    settle(part_in.at[1], sems.at[14])
    for k, offsets in enumerate(((7, 6, 5, 4), (3, 2, 1, 0))):
        product, extra = project(core, [at(chip, d) for d in offsets])
        to_sib[k].wait_recv()
        for i, d in enumerate(offsets):
            to = at(chip, d)
            c_out[d, :, :DDEP] = (product[i] + c_in_sib[d, :, :DDEP].astype(F32)).astype(BF16)
            c_out[d, :, DDEP:] = (extra[i] + c_in_sib[d, :, DDEP:].astype(F32)).astype(BF16)
            if d:
                remote(c_out.at[d], c_in.at[d - 1], sems.at[19], sems.at[20], (to * 2 + core, t)).start()
    settle(look_in, sems.at[16])
    looked = look_out[chip].astype(F32)
    for d in range(CHIPS - 1):
        looked = looked + look_in[d].astype(F32)
    summed = c_out[0].astype(F32)
    settle(c_in, sems.at[20])
    for d in range(CHIPS - 1):
        summed = summed + c_in[d].astype(F32)
    squares = jnp.sum(summed[:, DDEP:], axis=1, keepdims=True)
    depth_in = summed[:, :DDEP] * lax.rsqrt(squares / D + EPS) + looked

    dgain_load.wait()
    mean_sq = jnp.mean(depth_in * depth_in, axis=1, keepdims=True)
    normed = (depth_in * lax.rsqrt(mean_sq + EPS) * dgain[...]).astype(BF16)
    dqkv_load.wait()
    for e in (2, 1, 3, 0):
        to = (col + e) % 4
        for p in range(3):
            first = pl.multiple_of(p * DDEP + to * QUAD, QUAD)
            d_out[e, :, p * QUAD : (p + 1) * QUAD] = dot(normed, dqkv[:, pl.ds(first, QUAD)]).astype(BF16)

        @pl.when(row == 0)
        def _(e=e, to=to):
            remote(
                d_out.at[e, :, QUAD:], d_in.at[t, :, QUAD:], sems.at[21], sems.at[22], (s, 4 + to)
            ).start()

        if e:
            remote(d_out.at[e], d_in.at[t], sems.at[23], sems.at[24], (s, row * 4 + to)).start()
    d_in[t] = d_out[0]
    settle(d_in.at[pl.ds(0, 3)], sems.at[24])

    head_r = lax.broadcasted_iota(jnp.int32, (QUAD, QUAD), 0) // DH
    head_c = lax.broadcasted_iota(jnp.int32, (QUAD, QUAD), 1) // DH
    same_head = jnp.where(head_r == head_c, 1.0, 0.0).astype(BF16)

    def attend(codebooks):
        count = codebooks[-1] + 1
        qs = [d_in[c, :, :QUAD].astype(F32) for c in codebooks]
        ks = [d_in[c, :, QUAD : 2 * QUAD].astype(F32) for c in range(count)]
        vs = [d_in[c, :, 2 * QUAD :].astype(F32) for c in range(count)]
        products = jnp.concatenate(
            [qs[i] * ks[j] for i, c in enumerate(codebooks) for j in range(c + 1)], axis=0
        )
        high = products.astype(BF16)
        low = (products - high.astype(F32)).astype(BF16)
        scores = (dot(high, same_head) + dot(low, same_head)) * DH ** (-0.5)
        start = 0
        for i, c in enumerate(codebooks):
            lines = [scores[(start + j) * ROWS : (start + j + 1) * ROWS] for j in range(c + 1)]
            start += c + 1
            top = lines[0]
            for line in lines[1:]:
                top = jnp.maximum(top, line)
            total = jnp.zeros((ROWS, QUAD), F32)
            context = jnp.zeros((ROWS, QUAD), F32)
            for j, line in enumerate(lines):
                weight = jnp.exp(line - top)
                total = total + weight
                context = context + weight * vs[j]
            e_out[i] = (context / total).astype(BF16)

    @pl.when(row == 0)
    def _():
        attend((0, 1, 2, 3))

    @pl.when(row == 1)
    def _():
        settle(d_in.at[pl.ds(0, 4), :, QUAD:], sems.at[22])
        attend((4, 5, 6, 7))

    for e in (2, 1, 3):
        to = (col + e) % 4
        remote(e_out.at[to], e_in.at[col], sems.at[25], sems.at[26], (s, row * 4 + to)).start()
    e_in[col] = e_out[col]
    dout_load.wait()
    settle(e_in.at[pl.ds(0, 3)], sems.at[26])
    context = jnp.concatenate([e_in[i] for i in range(4)], axis=1)
    out_ref[...] = (depth_in + dot(context, dout[...])).astype(BF16)

    for ref, i in (
        (look_sib, 0),
        (look_in, 2),
        (look_in, 3),
        (look_in.at[0], 5),
        (part_in.at[0], 7),
        (part_in.at[1], 8),
        (part_in.at[0], 11),
        (part_in.at[1], 12),
        (look_in, 15),
        (c_sib, 17),
        (c_in, 19),
        (d_in.at[pl.ds(0, 3)], 23),
        (e_in.at[pl.ds(0, 3)], 25),
    ):
        settle(ref, sems.at[i])

    @pl.when(row == 0)
    def _():
        settle(d_in.at[pl.ds(0, 4), :, QUAD:], sems.at[21])


def shards(
    x_resid,
    qkv_new,
    kv_cache,
    cache_lens,
    wo_temporal,
    norm_gain,
    w_in,
    embed_rows,
    token_ids,
    depth_gain,
    depth_qkv,
    depth_out,
):
    args = (
        x_resid,
        qkv_new.reshape(ROWS, (GROUP + 2) * HD),
        kv_cache.reshape(ROWS, 2, FRAMES, HD),
        cache_lens,
        wo_temporal,
        norm_gain.reshape(1, COLS),
        w_in.reshape(COLS, DDEP),
        embed_rows.reshape(128, DDEP),
        token_ids.reshape(1, 256),
        depth_gain,
        depth_qkv.reshape(DDEP, 3 * DDEP),
        depth_out.reshape(DDEP, DDEP),
    )
    args = tuple(pltpu.with_memory_space_constraint(a, pltpu.HBM) for a in args)
    dma = pltpu.SemaphoreType.DMA
    vm = pltpu.VMEM
    out = pl.pallas_call(
        frame_kernel,
        name="frame",
        out_shape=jax.ShapeDtypeStruct((ROWS, DDEP), BF16),
        in_specs=[pl.BlockSpec(memory_space=pltpu.HBM)] * len(args),
        out_specs=pl.BlockSpec(memory_space=pltpu.VMEM),
        scratch_shapes=[
            vm((ROWS, FRAMES, HD), BF16),
            vm((ROWS, FRAMES, HD), BF16),
            vm((GROUP * HD, COLS), BF16),
            vm((COLS, DDEP), BF16),
            vm((128, DDEP), BF16),
            vm((DDEP, 3 * DDEP), BF16),
            vm((DDEP, DDEP), BF16),
            vm((32, COLS), BF16),
            vm((ROWS, (GROUP + 2) * HD), BF16),
            pltpu.SMEM((ROWS,), jnp.int32),
            vm((1, COLS), F32),
            vm((1, DDEP), F32),
            vm((1, 256), jnp.int32),
            dma((6,)),
            dma((11,)),
            vm((ROWS * GROUP, HD), F32),
            vm((ROWS * GROUP, HD), F32),
            vm((ROWS * GROUP, HD), F32),
            vm((2, ROWS * HD, HD), BF16),
            vm((HD, HALF_FRAMES), F32),
            vm((ROWS * GROUP, HD), F32),
            vm((2, CHIPS, 2, ROWS, GROUP * HD // 2), BF16),
            vm((2, TP, ROWS, COLS), BF16),
            vm((2, TP - 1, ROWS, COLS), BF16),
            vm((TP, 2, ROWS, COLS), BF16),
            vm((CHIPS, 2, ROWS, 128), BF16),
            vm((CHIPS, ROWS, DDEP), BF16),
            vm((CHIPS, ROWS, DDEP), BF16),
            vm((CHIPS, ROWS, DDEP), BF16),
            vm((CHIPS, ROWS, DDEP), BF16),
            vm((CHIPS - 1, ROWS, DDEP), BF16),
            vm((CHIPS, ROWS, WIDE), BF16),
            vm((CHIPS, ROWS, WIDE), BF16),
            vm((CHIPS, ROWS, WIDE), BF16),
            vm((CHIPS - 1, ROWS, WIDE), BF16),
            vm((4, ROWS, 3 * QUAD), BF16),
            vm((TP, ROWS, 3 * QUAD), BF16),
            vm((4, ROWS, QUAD), BF16),
            vm((4, ROWS, QUAD), BF16),
            dma((14,)),
            dma((28,)),
        ],
        compiler_params=pltpu.CompilerParams(
            collective_id=0, has_side_effects=True, vmem_limit_bytes=40 * 2**20
        ),
        cost_estimate=pl.CostEstimate(flops=10**9, bytes_accessed=19 * 10**6, transcendentals=10**5),
    )(*args)
    return out.reshape(ROWS, 1, DDEP)


def solution(mesh):
    in_specs = (
        P(None, "sess"),
        P("sess", "tp", None),
        P("sess", None, "tp", None, None),
        P("sess"),
        P("tp", "sess"),
        P("sess"),
        P("tp", "sess", None),
        P("tp", "sess", None),
        P(None, "tp"),
        P("tp", None),
        P("tp", None, None),
        P("tp", None, None),
    )
    out_specs = P("sess", "tp", None)
    return jax.shard_map(shards, mesh=mesh, in_specs=in_specs, out_specs=out_specs, check_vma=False)
```

```python
import jax
import jax.numpy as jnp
from jax import lax
from jax.experimental import pallas as pl
from jax.experimental.pallas import tpu as pltpu
from jax.sharding import PartitionSpec as P

MESH = pl.DeviceIdType.MESH
F32 = jnp.float32
BF16 = jnp.bfloat16

D = 8192
EPS = 1e-05
CHIPS = 8
TP = 8
ROWS = 16
GROUP = 8
HD = 128
FRAMES = 1024
COLS = 512
DDEP = 1024
WIDE = DDEP + 128
QUAD = 256
DH = 64
HALF = 8
HALF_FRAMES = FRAMES // 2


def dot(a, b):
    return jnp.dot(a, b, preferred_element_type=F32)


def frame_kernel(
    x_hbm,
    qkv_hbm,
    kv_hbm,
    lens_hbm,
    wo_hbm,
    gain_hbm,
    win_hbm,
    emb_hbm,
    tok_hbm,
    dgain_hbm,
    dqkv_hbm,
    dout_hbm,
    out_ref,
    keys,
    values,
    wo,
    win,
    emb,
    dqkv,
    dout,
    xres,
    qkv,
    lens,
    gain,
    dgain,
    tok,
    kv_sem,
    in_sem,
    q_scr,
    k_scr,
    v_scr,
    query_cols,
    weight_scr,
    o_scr,
    attn_all,
    part,
    part_in,
    hid_all,
    onehot,
    look_own,
    look_sib,
    look_in_sib,
    look_out,
    look_in,
    c_sib,
    c_in_sib,
    c_out,
    c_in,
    d_out,
    d_in,
    e_out,
    e_in,
    direct_sem,
    sems,
):
    s = lax.axis_index("sess")
    t = lax.axis_index("tp")
    chip = s // 2
    core = s % 2
    other = 1 - core
    row = t // 4
    col = t % 4
    sibling = (chip * 2 + other, t)

    def step_of(d):
        return ((0, 0), (0, 1), (0, 3), (1, 0), (0, 2), (1, 1), (1, 3), (1, 2))[d]

    def at(i, d):
        hi, lo = step_of(d)
        return ((i // 4 + hi) % 2) * 4 + (i % 4 + lo) % 4

    def back(i, d):
        hi, lo = step_of(d)
        return ((i // 4 + hi) % 2) * 4 + (i % 4 + 4 - lo) % 4

    far_first = (7, 6, 5, 4, 3, 2, 1)
    near_first = (1, 2, 3, 4, 5, 6, 7)

    def remote(src, dst, send, recv, device):
        return pltpu.make_async_remote_copy(
            src_ref=src,
            dst_ref=dst,
            send_sem=send,
            recv_sem=recv,
            device_id=device,
            device_id_type=MESH,
        )

    def settle(ref, sem):
        pltpu.make_async_copy(ref, ref, sem).wait()

    def load(i, src, dst):
        return pltpu.make_async_copy(src, dst, in_sem.at[i])

    x_load = load(0, x_hbm.at[pl.ds(pl.multiple_of(t * 32, 32), 32)], xres)
    qkv_load = load(1, qkv_hbm, qkv)
    lens_load = load(2, lens_hbm, lens)
    gain_load = load(3, gain_hbm, gain)
    dgain_load = load(4, dgain_hbm, dgain)
    tok_load = load(5, tok_hbm, tok)
    emb_load = load(6, emb_hbm, emb)
    wo_load = load(7, wo_hbm, wo)
    win_load = load(8, win_hbm, win)
    dqkv_load = load(9, dqkv_hbm, dqkv)
    dout_load = load(10, dout_hbm, dout)
    def cache_load(which, first, count, dst, i):
        part_of = pl.ds(first, count)
        return pltpu.make_async_copy(kv_hbm.at[part_of, which], dst.at[part_of], kv_sem.at[i])

    key_loads = [cache_load(0, a * HALF, HALF, keys, a) for a in range(2)]
    value_loads = [cache_load(1, g * 4, 4, values, 2 + g) for g in range(4)]
    loads = [qkv_load, key_loads[0], lens_load, value_loads[0], value_loads[1], key_loads[1], value_loads[2], value_loads[3]]
    for copy in loads:
        copy.start()

    barrier = pltpu.get_barrier_semaphore()
    pl.semaphore_signal(barrier, inc=1, device_id=sibling, device_id_type=MESH)
    for d in far_first:
        for device in ((at(chip, d) * 2, t), (at(chip, d) * 2 + 1, t), (s, at(t, d))):
            pl.semaphore_signal(barrier, inc=1, device_id=device, device_id_type=MESH)
    for copy in (tok_load, emb_load, gain_load, dgain_load, x_load):
        copy.start()

    qkv_load.wait()
    new_keys = qkv[:, GROUP * HD : (GROUP + 1) * HD].astype(F32)
    new_values = qkv[:, (GROUP + 1) * HD :].astype(F32)
    for h in range(GROUP):
        rows_h = pl.ds(h, ROWS, stride=GROUP)
        q_scr[rows_h, :] = qkv[:, h * HD : (h + 1) * HD].astype(F32)
        k_scr[rows_h, :] = new_keys
        v_scr[rows_h, :] = new_values
    query_t = q_scr[...].T
    scale = HD ** (-0.5)
    new_score = jnp.sum(query_t * k_scr[...].T, axis=0, keepdims=True) * scale
    new_score = jnp.broadcast_to(new_score, (8, HD))
    column = lax.broadcasted_iota(jnp.int32, (HD, HD), 1)
    line = lax.broadcasted_iota(jnp.int32, (8, HD), 1)
    swapped = pltpu.roll(query_t, 64, 1)
    swapped_score = pltpu.roll(new_score, 64, 1)
    lens_load.wait()
    half_scores = []
    lives = []
    for a in range(2):
        half_query = jnp.where((column < 64) == (a == 0), query_t, swapped)
        half_scores.append(jnp.where((line < 64) == (a == 0), new_score, swapped_score))
        live = jnp.zeros((8, HD), jnp.int32)
        for i in range(HALF):
            live = jnp.where((line // GROUP) % HALF == i, lens[a * HALF + i], live)
            for f in range(2):
                block = f * HALF + i
                query_cols[a, block * HD : (block + 1) * HD, :] = jnp.where(
                    column // GROUP == block, half_query, 0.0
                ).astype(BF16)
        lives.append(live - jnp.where(line < 64, 0, HALF_FRAMES))
    frame = lax.broadcasted_iota(jnp.int32, (HALF_FRAMES, HD), 0)

    def attend_half(a):
        key_loads[a].wait()
        joined = jnp.concatenate(
            [
                keys[a * HALF + i, f * HALF_FRAMES : (f + 1) * HALF_FRAMES]
                for f in range(2)
                for i in range(HALF)
            ],
            axis=1,
        )
        scores = dot(joined, query_cols[a]) * scale
        masked = jnp.where(frame < lives[a][:1], scores, -1e30)
        top = jnp.broadcast_to(jnp.max(masked, axis=0, keepdims=True), (8, HD))
        peak = jnp.maximum(jnp.maximum(top, pltpu.roll(top, 64, 1)), half_scores[a])
        expo = jnp.exp(masked - peak[:1])
        new_expo = jnp.exp(half_scores[a] - peak)
        total = jnp.broadcast_to(jnp.sum(expo, axis=0, keepdims=True), (8, HD))
        inv = 1.0 / (total + pltpu.roll(total, 64, 1) + new_expo)
        weight_scr[...] = (expo * inv[:1]).T
        new_weight = (new_expo * inv).astype(BF16).astype(F32)
        new_column = jnp.broadcast_to(new_weight[:1], (HD, HD)).T
        for g in range(2):
            value_loads[a * 2 + g].wait()
            for i in range(g * 4, g * 4 + 4, 2):
                session = a * HALF + i
                context = None
                for f in range(2):
                    rows_f = slice(f * 64 + i * GROUP, f * 64 + (i + 2) * GROUP)
                    frames = slice(f * HALF_FRAMES, (f + 1) * HALF_FRAMES)
                    pair = jnp.concatenate([values[session, frames], values[session + 1, frames]], axis=1)
                    partial = dot(weight_scr[rows_f, :].astype(BF16), pair)
                    context = partial if f == 0 else context + partial
                rows_i = slice(i * GROUP, (i + 2) * GROUP)
                rows_s = slice(session * GROUP, (session + 2) * GROUP)
                own = jnp.concatenate([context[:GROUP, :HD], context[GROUP:, HD:]], axis=0)
                o_scr[rows_s, :] = own + new_column[rows_i] * v_scr[rows_s, :]

    gather = {}

    def gather_half(a):
        for h in range(4):
            low_heads = o_scr[pl.ds(a * 64 + h, HALF, stride=GROUP), :]
            high_heads = o_scr[pl.ds(a * 64 + h + 4, HALF, stride=GROUP), :]
            attn_all[a, chip, core, :, h * HD : (h + 1) * HD] = jnp.concatenate(
                [low_heads, high_heads], axis=0
            ).astype(BF16)
        mine = attn_all.at[a, chip, core]
        if a == 0:
            pl.semaphore_wait(barrier, 22)
        for d in far_first:
            gather[a, d] = remote(
                mine, mine, sems.at[2], direct_sem.at[a * 7 + d - 1], (at(chip, d) * 2 + other, t)
            )
            gather[a, d].start()
            if d == 7:
                remote(mine, mine, sems.at[3], sems.at[4], (at(chip, d) * 2 + core, t)).start()
        remote(mine, mine, sems.at[5], sems.at[6], sibling).start()

    attend_half(0)
    gather_half(0)
    wo_load.start()
    win_load.start()
    attend_half(1)
    gather_half(1)
    dqkv_load.start()
    dout_load.start()

    tok_load.wait()
    emb_load.wait()
    entry = lax.broadcasted_iota(jnp.int32, (128, 256), 0) + s * 128
    hot = jnp.where(tok[...] == entry, 1.0, 0.0).T.astype(BF16)
    onehot[...] = hot.reshape(CHIPS, 2, ROWS, 128)

    def look(parity):
        rows = onehot[:, pl.ds(parity, 1)].reshape(CHIPS * ROWS, 128)
        return dot(rows, emb[...]).astype(BF16).reshape(CHIPS, ROWS, DDEP)

    look_sib[...] = look(other)
    look_to_sib = remote(look_sib, look_in_sib, sems.at[0], sems.at[1], sibling)
    look_to_sib.start()
    look_own[...] = look(core)

    gain_load.wait()
    win_load.wait()
    gain_col = jnp.broadcast_to(gain[...], (128, COLS)).T
    for j in range(DDEP // 128):
        cols = slice(j * 128, (j + 1) * 128)
        win[:, cols] = (win[:, cols].astype(F32) * gain_col).astype(BF16)

    for a in range(2):
        for d in near_first:
            gather[a, d].wait_recv()
            if d < 7:
                block = attn_all.at[a, back(chip, d), other]
                remote(block, block, sems.at[3], sems.at[4], sibling).start()
    settle(look_in.at[0], sems.at[6])
    wo_load.wait()

    def attention_rows(parity, chips):
        blocks = []
        for i in chips:
            for a in range(2):
                block = attn_all[a, i, parity].astype(F32)
                blocks.append(jnp.concatenate([block[:HALF], block[HALF:]], axis=1))
        return jnp.concatenate(blocks, axis=0).astype(BF16)

    def reduce_start(half, parity):
        for offsets in ((7, 6, 5, 4), (3, 2, 1, 0)):
            rows = attention_rows(parity, [at(t, d) for d in offsets])
            product = dot(rows, wo[...]).astype(BF16).reshape(4, ROWS, COLS)
            for i, d in enumerate(offsets):
                part[half, d] = product[i]
                if d:
                    remote(
                        part.at[half, d], part_in.at[half, d - 1], sems.at[7 + half], sems.at[9 + half], (s, at(t, d))
                    ).start()

    reduce_start(0, other)
    settle(look_in, sems.at[4])
    reduce_start(1, core)
    look_to_sib.wait_recv()
    look_out[...] = (look_own[...].astype(F32) + look_in_sib[...].astype(F32)).astype(BF16)
    for d in far_first:
        to = at(chip, d)
        remote(look_out.at[to], look_in.at[d - 1], sems.at[15], sems.at[16], (to * 2 + core, t)).start()
    x_load.wait()

    def gather_start(half, parity):
        hidden = xres[pl.ds(pl.multiple_of(parity * ROWS, ROWS), ROWS)].astype(F32) + part[half, 0].astype(F32)
        settle(part_in.at[half], sems.at[9 + half])
        for d in range(CHIPS - 1):
            hidden = hidden + part_in[half, d].astype(F32)
        hid_all[t, parity] = hidden.astype(BF16)
        block = hid_all.at[t, parity]
        for d in far_first:
            remote(block, block, sems.at[11 + half], sems.at[13 + half], (s, at(t, d))).start()

    gather_start(0, other)
    gather_start(1, core)

    lane = lax.broadcasted_iota(jnp.int32, (4 * ROWS, 128), 1)

    def project(parity, blocks):
        rows = jnp.concatenate([hid_all[i, parity] for i in blocks], axis=0)
        wide = rows.astype(F32)
        squares = jnp.sum(wide * wide, axis=1, keepdims=True)
        high = squares.astype(BF16).astype(F32)
        low = squares - high
        extra = jnp.where(lane == 2 * core, high, 0.0) + jnp.where(lane == 2 * core + 1, low, 0.0)
        return dot(rows, win[...]).reshape(len(blocks), ROWS, DDEP), extra.reshape(len(blocks), ROWS, 128)

    settle(part_in.at[0], sems.at[13])
    to_sib = {}
    for k, offsets in enumerate(((7, 6, 5, 4), (3, 2, 1, 0))):
        product, extra = project(other, [at(chip, d) for d in offsets])
        for i, d in enumerate(offsets):
            c_sib[d, :, :DDEP] = product[i].astype(BF16)
            c_sib[d, :, DDEP:] = extra[i].astype(BF16)
        part_of = pl.ds(offsets[3], 4)
        to_sib[k] = remote(
            c_sib.at[part_of], c_in_sib.at[part_of], sems.at[17], sems.at[18 if k == 0 else 27], sibling
        )
        to_sib[k].start()
    settle(part_in.at[1], sems.at[14])
    for k, offsets in enumerate(((7, 6, 5, 4), (3, 2, 1, 0))):
        product, extra = project(core, [at(chip, d) for d in offsets])
        to_sib[k].wait_recv()
        for i, d in enumerate(offsets):
            to = at(chip, d)
            c_out[d, :, :DDEP] = (product[i] + c_in_sib[d, :, :DDEP].astype(F32)).astype(BF16)
            c_out[d, :, DDEP:] = (extra[i] + c_in_sib[d, :, DDEP:].astype(F32)).astype(BF16)
            if d:
                remote(c_out.at[d], c_in.at[d - 1], sems.at[19], sems.at[20], (to * 2 + core, t)).start()
    settle(look_in, sems.at[16])
    looked = look_out[chip].astype(F32)
    for d in range(CHIPS - 1):
        looked = looked + look_in[d].astype(F32)
    summed = c_out[0].astype(F32)
    settle(c_in, sems.at[20])
    for d in range(CHIPS - 1):
        summed = summed + c_in[d].astype(F32)
    squares = jnp.sum(summed[:, DDEP:], axis=1, keepdims=True)
    depth_in = summed[:, :DDEP] * lax.rsqrt(squares / D + EPS) + looked

    dgain_load.wait()
    mean_sq = jnp.mean(depth_in * depth_in, axis=1, keepdims=True)
    normed = (depth_in * lax.rsqrt(mean_sq + EPS) * dgain[...]).astype(BF16)
    dqkv_load.wait()
    for e in (2, 1, 3, 0):
        to = (col + e) % 4
        for p in range(3):
            first = pl.multiple_of(p * DDEP + to * QUAD, QUAD)
            d_out[e, :, p * QUAD : (p + 1) * QUAD] = dot(normed, dqkv[:, pl.ds(first, QUAD)]).astype(BF16)

        @pl.when(row == 0)
        def _(e=e, to=to):
            remote(
                d_out.at[e, :, QUAD:], d_in.at[t, :, QUAD:], sems.at[21], sems.at[22], (s, 4 + to)
            ).start()

        if e:
            remote(d_out.at[e], d_in.at[t], sems.at[23], sems.at[24], (s, row * 4 + to)).start()
    d_in[t] = d_out[0]
    settle(d_in.at[pl.ds(0, 3)], sems.at[24])

    head_r = lax.broadcasted_iota(jnp.int32, (QUAD, QUAD), 0) // DH
    head_c = lax.broadcasted_iota(jnp.int32, (QUAD, QUAD), 1) // DH
    same_head = jnp.where(head_r == head_c, 1.0, 0.0).astype(BF16)

    def attend(codebooks):
        count = codebooks[-1] + 1
        qs = [d_in[c, :, :QUAD].astype(F32) for c in codebooks]
        ks = [d_in[c, :, QUAD : 2 * QUAD].astype(F32) for c in range(count)]
        vs = [d_in[c, :, 2 * QUAD :].astype(F32) for c in range(count)]
        products = jnp.concatenate(
            [qs[i] * ks[j] for i, c in enumerate(codebooks) for j in range(c + 1)], axis=0
        )
        high = products.astype(BF16)
        low = (products - high.astype(F32)).astype(BF16)
        scores = (dot(high, same_head) + dot(low, same_head)) * DH ** (-0.5)
        start = 0
        for i, c in enumerate(codebooks):
            lines = [scores[(start + j) * ROWS : (start + j + 1) * ROWS] for j in range(c + 1)]
            start += c + 1
            top = lines[0]
            for line in lines[1:]:
                top = jnp.maximum(top, line)
            total = jnp.zeros((ROWS, QUAD), F32)
            context = jnp.zeros((ROWS, QUAD), F32)
            for j, line in enumerate(lines):
                weight = jnp.exp(line - top)
                total = total + weight
                context = context + weight * vs[j]
            e_out[i] = (context / total).astype(BF16)

    @pl.when(row == 0)
    def _():
        attend((0, 1, 2, 3))

    @pl.when(row == 1)
    def _():
        settle(d_in.at[pl.ds(0, 4), :, QUAD:], sems.at[22])
        attend((4, 5, 6, 7))

    back_copies = {}
    for k, e in enumerate((2, 1, 3)):
        to = (col + e) % 4
        back_copies[e] = remote(e_out.at[to], e_in.at[e], sems.at[25], sems.at[(26, 28, 29)[k]], (s, row * 4 + to))
        back_copies[e].start()

    def project_out(block, source):
        first = pl.multiple_of(source * QUAD, QUAD)
        return dot(block, dout[pl.ds(first, QUAD), :])

    dout_load.wait()
    result = depth_in + project_out(e_out[col], col)
    for e in (1, 3, 2):
        back_copies[e].wait_recv()
        result = result + project_out(e_in[e], (col + 4 - e) % 4)
    out_ref[...] = result.astype(BF16)

    for ref, i in (
        (look_sib, 0),
        (look_in, 2),
        (look_in, 3),
        (look_in.at[0], 5),
        (part_in.at[0], 7),
        (part_in.at[1], 8),
        (part_in.at[0], 11),
        (part_in.at[1], 12),
        (look_in, 15),
        (c_sib, 17),
        (c_in, 19),
        (d_in.at[pl.ds(0, 3)], 23),
        (e_in.at[pl.ds(0, 3)], 25),
    ):
        settle(ref, sems.at[i])

    @pl.when(row == 0)
    def _():
        settle(d_in.at[pl.ds(0, 4), :, QUAD:], sems.at[21])


def shards(
    x_resid,
    qkv_new,
    kv_cache,
    cache_lens,
    wo_temporal,
    norm_gain,
    w_in,
    embed_rows,
    token_ids,
    depth_gain,
    depth_qkv,
    depth_out,
):
    args = (
        x_resid,
        qkv_new.reshape(ROWS, (GROUP + 2) * HD),
        kv_cache.reshape(ROWS, 2, FRAMES, HD),
        cache_lens,
        wo_temporal,
        norm_gain.reshape(1, COLS),
        w_in.reshape(COLS, DDEP),
        embed_rows.reshape(128, DDEP),
        token_ids.reshape(1, 256),
        depth_gain,
        depth_qkv.reshape(DDEP, 3 * DDEP),
        depth_out.reshape(DDEP, DDEP),
    )
    args = tuple(pltpu.with_memory_space_constraint(a, pltpu.HBM) for a in args)
    dma = pltpu.SemaphoreType.DMA
    vm = pltpu.VMEM
    out = pl.pallas_call(
        frame_kernel,
        name="frame",
        out_shape=jax.ShapeDtypeStruct((ROWS, DDEP), BF16),
        in_specs=[pl.BlockSpec(memory_space=pltpu.HBM)] * len(args),
        out_specs=pl.BlockSpec(memory_space=pltpu.VMEM),
        scratch_shapes=[
            vm((ROWS, FRAMES, HD), BF16),
            vm((ROWS, FRAMES, HD), BF16),
            vm((GROUP * HD, COLS), BF16),
            vm((COLS, DDEP), BF16),
            vm((128, DDEP), BF16),
            vm((DDEP, 3 * DDEP), BF16),
            vm((DDEP, DDEP), BF16),
            vm((32, COLS), BF16),
            vm((ROWS, (GROUP + 2) * HD), BF16),
            pltpu.SMEM((ROWS,), jnp.int32),
            vm((1, COLS), F32),
            vm((1, DDEP), F32),
            vm((1, 256), jnp.int32),
            dma((6,)),
            dma((11,)),
            vm((ROWS * GROUP, HD), F32),
            vm((ROWS * GROUP, HD), F32),
            vm((ROWS * GROUP, HD), F32),
            vm((2, ROWS * HD, HD), BF16),
            vm((HD, HALF_FRAMES), F32),
            vm((ROWS * GROUP, HD), F32),
            vm((2, CHIPS, 2, ROWS, GROUP * HD // 2), BF16),
            vm((2, TP, ROWS, COLS), BF16),
            vm((2, TP - 1, ROWS, COLS), BF16),
            vm((TP, 2, ROWS, COLS), BF16),
            vm((CHIPS, 2, ROWS, 128), BF16),
            vm((CHIPS, ROWS, DDEP), BF16),
            vm((CHIPS, ROWS, DDEP), BF16),
            vm((CHIPS, ROWS, DDEP), BF16),
            vm((CHIPS, ROWS, DDEP), BF16),
            vm((CHIPS - 1, ROWS, DDEP), BF16),
            vm((CHIPS, ROWS, WIDE), BF16),
            vm((CHIPS, ROWS, WIDE), BF16),
            vm((CHIPS, ROWS, WIDE), BF16),
            vm((CHIPS - 1, ROWS, WIDE), BF16),
            vm((4, ROWS, 3 * QUAD), BF16),
            vm((TP, ROWS, 3 * QUAD), BF16),
            vm((4, ROWS, QUAD), BF16),
            vm((4, ROWS, QUAD), BF16),
            dma((14,)),
            dma((30,)),
        ],
        compiler_params=pltpu.CompilerParams(
            collective_id=0, has_side_effects=True, vmem_limit_bytes=40 * 2**20
        ),
        cost_estimate=pl.CostEstimate(flops=10**9, bytes_accessed=19 * 10**6, transcendentals=10**5),
    )(*args)
    return out.reshape(ROWS, 1, DDEP)


def solution(mesh):
    in_specs = (
        P(None, "sess"),
        P("sess", "tp", None),
        P("sess", None, "tp", None, None),
        P("sess"),
        P("tp", "sess"),
        P("sess"),
        P("tp", "sess", None),
        P("tp", "sess", None),
        P(None, "tp"),
        P("tp", None),
        P("tp", None, None),
        P("tp", None, None),
    )
    out_specs = P("sess", "tp", None)
    return jax.shard_map(shards, mesh=mesh, in_specs=in_specs, out_specs=out_specs, check_vma=False)
```

```python
import jax
import jax.numpy as jnp
from jax import lax
from jax.experimental import pallas as pl
from jax.experimental.pallas import tpu as pltpu
from jax.sharding import PartitionSpec as P

MESH = pl.DeviceIdType.MESH
F32 = jnp.float32
BF16 = jnp.bfloat16

D = 8192
EPS = 1e-05
CHIPS = 8
TP = 8
ROWS = 16
GROUP = 8
HD = 128
FRAMES = 1024
COLS = 512
DDEP = 1024
WIDE = DDEP + 128
QUAD = 256
DH = 64
HALF = 8
HALF_FRAMES = FRAMES // 2


def dot(a, b):
    return jnp.dot(a, b, preferred_element_type=F32)


def frame_kernel(
    x_hbm,
    qkv_hbm,
    kv_hbm,
    lens_hbm,
    wo_hbm,
    gain_hbm,
    win_hbm,
    emb_hbm,
    tok_hbm,
    dgain_hbm,
    dqkv_hbm,
    dout_hbm,
    out_ref,
    keys,
    values,
    wo,
    win,
    emb,
    dqkv,
    dout,
    xres,
    qkv,
    lens,
    gain,
    dgain,
    tok,
    kv_sem,
    in_sem,
    q_scr,
    k_scr,
    v_scr,
    query_cols,
    weight_scr,
    o_scr,
    attn_all,
    part,
    part_in,
    hid_all,
    onehot,
    look_own,
    look_sib,
    look_in_sib,
    look_out,
    look_in,
    c_sib,
    c_in_sib,
    c_out,
    c_in,
    d_out,
    d_in,
    e_out,
    e_in,
    direct_sem,
    sems,
):
    s = lax.axis_index("sess")
    t = lax.axis_index("tp")
    chip = s // 2
    core = s % 2
    other = 1 - core
    row = t // 4
    col = t % 4
    sibling = (chip * 2 + other, t)

    def step_of(d):
        return ((0, 0), (0, 1), (0, 3), (1, 0), (0, 2), (1, 1), (1, 3), (1, 2))[d]

    def at(i, d):
        hi, lo = step_of(d)
        return ((i // 4 + hi) % 2) * 4 + (i % 4 + lo) % 4

    def back(i, d):
        hi, lo = step_of(d)
        return ((i // 4 + hi) % 2) * 4 + (i % 4 + 4 - lo) % 4

    far_first = (7, 6, 5, 4, 3, 2, 1)
    near_first = (1, 2, 3, 4, 5, 6, 7)

    def remote(src, dst, send, recv, device):
        return pltpu.make_async_remote_copy(
            src_ref=src,
            dst_ref=dst,
            send_sem=send,
            recv_sem=recv,
            device_id=device,
            device_id_type=MESH,
        )

    def settle(ref, sem):
        pltpu.make_async_copy(ref, ref, sem).wait()

    def load(i, src, dst):
        return pltpu.make_async_copy(src, dst, in_sem.at[i])

    x_load = load(0, x_hbm.at[pl.ds(pl.multiple_of(t * 32, 32), 32)], xres)
    qkv_load = load(1, qkv_hbm, qkv)
    lens_load = load(2, lens_hbm, lens)
    gain_load = load(3, gain_hbm, gain)
    dgain_load = load(4, dgain_hbm, dgain)
    tok_load = load(5, tok_hbm, tok)
    emb_load = load(6, emb_hbm, emb)
    wo_load = load(7, wo_hbm, wo)
    win_load = load(8, win_hbm, win)
    dqkv_load = load(9, dqkv_hbm, dqkv)
    dout_load = load(10, dout_hbm, dout)
    def cache_load(which, first, count, dst, i):
        part_of = pl.ds(first, count)
        return pltpu.make_async_copy(kv_hbm.at[part_of, which], dst.at[part_of], kv_sem.at[i])

    key_loads = [cache_load(0, a * HALF, HALF, keys, a) for a in range(2)]
    value_loads = [cache_load(1, g * 4, 4, values, 2 + g) for g in range(4)]
    loads = [qkv_load, key_loads[0], lens_load, value_loads[0], value_loads[1], key_loads[1], value_loads[2], value_loads[3]]
    for copy in loads:
        copy.start()

    barrier = pltpu.get_barrier_semaphore()
    pl.semaphore_signal(barrier, inc=1, device_id=sibling, device_id_type=MESH)
    for d in far_first:
        for device in ((at(chip, d) * 2, t), (at(chip, d) * 2 + 1, t), (s, at(t, d))):
            pl.semaphore_signal(barrier, inc=1, device_id=device, device_id_type=MESH)
    for copy in (tok_load, emb_load, gain_load, dgain_load, x_load):
        copy.start()

    qkv_load.wait()
    new_keys = qkv[:, GROUP * HD : (GROUP + 1) * HD].astype(F32)
    new_values = qkv[:, (GROUP + 1) * HD :].astype(F32)
    for h in range(GROUP):
        rows_h = pl.ds(h, ROWS, stride=GROUP)
        q_scr[rows_h, :] = qkv[:, h * HD : (h + 1) * HD].astype(F32)
        k_scr[rows_h, :] = new_keys
        v_scr[rows_h, :] = new_values
    query_t = q_scr[...].T
    scale = HD ** (-0.5)
    new_score = jnp.sum(query_t * k_scr[...].T, axis=0, keepdims=True) * scale
    new_score = jnp.broadcast_to(new_score, (8, HD))
    column = lax.broadcasted_iota(jnp.int32, (HD, HD), 1)
    line = lax.broadcasted_iota(jnp.int32, (8, HD), 1)
    swapped = pltpu.roll(query_t, 64, 1)
    swapped_score = pltpu.roll(new_score, 64, 1)
    lens_load.wait()
    half_scores = []
    lives = []
    for a in range(2):
        half_query = jnp.where((column < 64) == (a == 0), query_t, swapped)
        half_scores.append(jnp.where((line < 64) == (a == 0), new_score, swapped_score))
        live = jnp.zeros((8, HD), jnp.int32)
        for i in range(HALF):
            live = jnp.where((line // GROUP) % HALF == i, lens[a * HALF + i], live)
            for f in range(2):
                block = f * HALF + i
                query_cols[a, block * HD : (block + 1) * HD, :] = jnp.where(
                    column // GROUP == block, half_query, 0.0
                ).astype(BF16)
        lives.append(live - jnp.where(line < 64, 0, HALF_FRAMES))
    frame = lax.broadcasted_iota(jnp.int32, (HALF_FRAMES, HD), 0)

    def attend_half(a):
        key_loads[a].wait()
        joined = jnp.concatenate(
            [
                keys[a * HALF + i, f * HALF_FRAMES : (f + 1) * HALF_FRAMES]
                for f in range(2)
                for i in range(HALF)
            ],
            axis=1,
        )
        scores = dot(joined, query_cols[a]) * scale
        masked = jnp.where(frame < lives[a][:1], scores, -1e30)
        top = jnp.broadcast_to(jnp.max(masked, axis=0, keepdims=True), (8, HD))
        peak = jnp.maximum(jnp.maximum(top, pltpu.roll(top, 64, 1)), half_scores[a])
        expo = jnp.exp(masked - peak[:1])
        new_expo = jnp.exp(half_scores[a] - peak)
        total = jnp.broadcast_to(jnp.sum(expo, axis=0, keepdims=True), (8, HD))
        inv = 1.0 / (total + pltpu.roll(total, 64, 1) + new_expo)
        weight_scr[...] = (expo * inv[:1]).T
        new_weight = (new_expo * inv).astype(BF16).astype(F32)
        new_column = jnp.broadcast_to(new_weight[:1], (HD, HD)).T
        for g in range(2):
            value_loads[a * 2 + g].wait()
            for i in range(g * 4, g * 4 + 4, 2):
                session = a * HALF + i
                context = None
                for f in range(2):
                    rows_f = slice(f * 64 + i * GROUP, f * 64 + (i + 2) * GROUP)
                    frames = slice(f * HALF_FRAMES, (f + 1) * HALF_FRAMES)
                    pair = jnp.concatenate([values[session, frames], values[session + 1, frames]], axis=1)
                    partial = dot(weight_scr[rows_f, :].astype(BF16), pair)
                    context = partial if f == 0 else context + partial
                rows_i = slice(i * GROUP, (i + 2) * GROUP)
                rows_s = slice(session * GROUP, (session + 2) * GROUP)
                own = jnp.concatenate([context[:GROUP, :HD], context[GROUP:, HD:]], axis=0)
                o_scr[rows_s, :] = own + new_column[rows_i] * v_scr[rows_s, :]

    gather = {}

    def gather_half(a):
        for h in range(4):
            low_heads = o_scr[pl.ds(a * 64 + h, HALF, stride=GROUP), :]
            high_heads = o_scr[pl.ds(a * 64 + h + 4, HALF, stride=GROUP), :]
            attn_all[a, chip, core, :, h * HD : (h + 1) * HD] = jnp.concatenate(
                [low_heads, high_heads], axis=0
            ).astype(BF16)
        mine = attn_all.at[a, chip, core]
        if a == 0:
            pl.semaphore_wait(barrier, 22)
        for d in far_first:
            gather[a, d] = remote(
                mine, mine, sems.at[2], direct_sem.at[a * 7 + d - 1], (at(chip, d) * 2 + other, t)
            )
            gather[a, d].start()
            if d == 7:
                remote(mine, mine, sems.at[3], sems.at[4], (at(chip, d) * 2 + core, t)).start()
        remote(mine, mine, sems.at[5], sems.at[6], sibling).start()

    attend_half(0)
    gather_half(0)
    wo_load.start()
    win_load.start()
    attend_half(1)
    gather_half(1)
    dqkv_load.start()
    dout_load.start()

    tok_load.wait()
    emb_load.wait()
    entry = lax.broadcasted_iota(jnp.int32, (128, 256), 0) + s * 128
    hot = jnp.where(tok[...] == entry, 1.0, 0.0).T.astype(BF16)
    onehot[...] = hot.reshape(CHIPS, 2, ROWS, 128)

    def look(parity):
        rows = onehot[:, pl.ds(parity, 1)].reshape(CHIPS * ROWS, 128)
        return dot(rows, emb[...]).astype(BF16).reshape(CHIPS, ROWS, DDEP)

    look_sib[...] = look(other)
    look_to_sib = remote(look_sib, look_in_sib, sems.at[0], sems.at[1], sibling)
    look_to_sib.start()
    look_own[...] = look(core)

    gain_load.wait()
    win_load.wait()
    gain_col = jnp.broadcast_to(gain[...], (128, COLS)).T
    for j in range(DDEP // 128):
        cols = slice(j * 128, (j + 1) * 128)
        win[:, cols] = (win[:, cols].astype(F32) * gain_col).astype(BF16)

    for a in range(2):
        for d in near_first:
            gather[a, d].wait_recv()
            if d < 7:
                block = attn_all.at[a, back(chip, d), other]
                remote(block, block, sems.at[3], sems.at[4], sibling).start()
    settle(look_in.at[0], sems.at[6])
    wo_load.wait()

    def attention_rows(parity, chips):
        blocks = []
        for i in chips:
            for a in range(2):
                block = attn_all[a, i, parity].astype(F32)
                blocks.append(jnp.concatenate([block[:HALF], block[HALF:]], axis=1))
        return jnp.concatenate(blocks, axis=0).astype(BF16)

    def reduce_start(half, parity):
        for offsets in ((7, 6, 5, 4), (3, 2, 1, 0)):
            rows = attention_rows(parity, [at(t, d) for d in offsets])
            product = dot(rows, wo[...]).astype(BF16).reshape(4, ROWS, COLS)
            for i, d in enumerate(offsets):
                part[half, d] = product[i]
                if d:
                    remote(
                        part.at[half, d], part_in.at[half, d - 1], sems.at[7 + half], sems.at[9 + half], (s, at(t, d))
                    ).start()

    reduce_start(0, other)
    settle(look_in, sems.at[4])
    reduce_start(1, core)
    x_load.wait()

    def gather_start(half, parity):
        hidden = xres[pl.ds(pl.multiple_of(parity * ROWS, ROWS), ROWS)].astype(F32) + part[half, 0].astype(F32)
        settle(part_in.at[half], sems.at[9 + half])
        for d in range(CHIPS - 1):
            hidden = hidden + part_in[half, d].astype(F32)
        hid_all[t, parity] = hidden.astype(BF16)
        block = hid_all.at[t, parity]
        for d in far_first:
            remote(block, block, sems.at[11 + half], sems.at[13 + half], (s, at(t, d))).start()

    gather_start(0, other)
    gather_start(1, core)
    look_to_sib.wait_recv()
    look_out[...] = (look_own[...].astype(F32) + look_in_sib[...].astype(F32)).astype(BF16)
    for d in far_first:
        to = at(chip, d)
        remote(look_out.at[to], look_in.at[d - 1], sems.at[15], sems.at[16], (to * 2 + core, t)).start()

    lane = lax.broadcasted_iota(jnp.int32, (4 * ROWS, 128), 1)

    def project(parity, blocks):
        rows = jnp.concatenate([hid_all[i, parity] for i in blocks], axis=0)
        wide = rows.astype(F32)
        squares = jnp.sum(wide * wide, axis=1, keepdims=True)
        high = squares.astype(BF16).astype(F32)
        low = squares - high
        extra = jnp.where(lane == 2 * core, high, 0.0) + jnp.where(lane == 2 * core + 1, low, 0.0)
        return dot(rows, win[...]).reshape(len(blocks), ROWS, DDEP), extra.reshape(len(blocks), ROWS, 128)

    settle(part_in.at[0], sems.at[13])
    to_sib = {}
    for k, offsets in enumerate(((7, 6, 5, 4), (3, 2, 1, 0))):
        product, extra = project(other, [at(chip, d) for d in offsets])
        for i, d in enumerate(offsets):
            c_sib[d, :, :DDEP] = product[i].astype(BF16)
            c_sib[d, :, DDEP:] = extra[i].astype(BF16)
        part_of = pl.ds(offsets[3], 4)
        to_sib[k] = remote(
            c_sib.at[part_of], c_in_sib.at[part_of], sems.at[17], sems.at[18 if k == 0 else 27], sibling
        )
        to_sib[k].start()
    settle(part_in.at[1], sems.at[14])
    for k, offsets in enumerate(((7, 6, 5, 4), (3, 2, 1, 0))):
        product, extra = project(core, [at(chip, d) for d in offsets])
        to_sib[k].wait_recv()
        for i, d in enumerate(offsets):
            to = at(chip, d)
            c_out[d, :, :DDEP] = (product[i] + c_in_sib[d, :, :DDEP].astype(F32)).astype(BF16)
            c_out[d, :, DDEP:] = (extra[i] + c_in_sib[d, :, DDEP:].astype(F32)).astype(BF16)
            if d:
                remote(c_out.at[d], c_in.at[d - 1], sems.at[19], sems.at[20], (to * 2 + core, t)).start()
    settle(look_in, sems.at[16])
    looked = look_out[chip].astype(F32)
    for d in range(CHIPS - 1):
        looked = looked + look_in[d].astype(F32)
    summed = c_out[0].astype(F32)
    settle(c_in, sems.at[20])
    for d in range(CHIPS - 1):
        summed = summed + c_in[d].astype(F32)
    squares = jnp.sum(summed[:, DDEP:], axis=1, keepdims=True)
    depth_in = summed[:, :DDEP] * lax.rsqrt(squares / D + EPS) + looked

    dgain_load.wait()
    mean_sq = jnp.mean(depth_in * depth_in, axis=1, keepdims=True)
    normed = (depth_in * lax.rsqrt(mean_sq + EPS) * dgain[...]).astype(BF16)
    dqkv_load.wait()
    for e in (2, 1, 3, 0):
        to = (col + e) % 4
        for p in range(3):
            first = pl.multiple_of(p * DDEP + to * QUAD, QUAD)
            d_out[e, :, p * QUAD : (p + 1) * QUAD] = dot(normed, dqkv[:, pl.ds(first, QUAD)]).astype(BF16)

        @pl.when(row == 0)
        def _(e=e, to=to):
            remote(
                d_out.at[e, :, QUAD:], d_in.at[t, :, QUAD:], sems.at[21], sems.at[22], (s, 4 + to)
            ).start()

        if e:
            remote(d_out.at[e], d_in.at[t], sems.at[23], sems.at[24], (s, row * 4 + to)).start()
    d_in[t] = d_out[0]
    settle(d_in.at[pl.ds(0, 3)], sems.at[24])

    head_r = lax.broadcasted_iota(jnp.int32, (QUAD, QUAD), 0) // DH
    head_c = lax.broadcasted_iota(jnp.int32, (QUAD, QUAD), 1) // DH
    same_head = jnp.where(head_r == head_c, 1.0, 0.0).astype(BF16)

    def attend(codebooks):
        count = codebooks[-1] + 1
        qs = [d_in[c, :, :QUAD].astype(F32) for c in codebooks]
        ks = [d_in[c, :, QUAD : 2 * QUAD].astype(F32) for c in range(count)]
        vs = [d_in[c, :, 2 * QUAD :].astype(F32) for c in range(count)]
        products = jnp.concatenate(
            [qs[i] * ks[j] for i, c in enumerate(codebooks) for j in range(c + 1)], axis=0
        )
        high = products.astype(BF16)
        low = (products - high.astype(F32)).astype(BF16)
        scores = (dot(high, same_head) + dot(low, same_head)) * DH ** (-0.5)
        start = 0
        for i, c in enumerate(codebooks):
            lines = [scores[(start + j) * ROWS : (start + j + 1) * ROWS] for j in range(c + 1)]
            start += c + 1
            top = lines[0]
            for line in lines[1:]:
                top = jnp.maximum(top, line)
            total = jnp.zeros((ROWS, QUAD), F32)
            context = jnp.zeros((ROWS, QUAD), F32)
            for j, line in enumerate(lines):
                weight = jnp.exp(line - top)
                total = total + weight
                context = context + weight * vs[j]
            e_out[i] = (context / total).astype(BF16)

    @pl.when(row == 0)
    def _():
        attend((0, 1, 2, 3))

    @pl.when(row == 1)
    def _():
        settle(d_in.at[pl.ds(0, 4), :, QUAD:], sems.at[22])
        attend((4, 5, 6, 7))

    back_copies = {}
    for k, e in enumerate((2, 1, 3)):
        to = (col + e) % 4
        back_copies[e] = remote(e_out.at[to], e_in.at[e], sems.at[25], sems.at[(26, 28, 29)[k]], (s, row * 4 + to))
        back_copies[e].start()

    def project_out(block, source):
        first = pl.multiple_of(source * QUAD, QUAD)
        return dot(block, dout[pl.ds(first, QUAD), :])

    dout_load.wait()
    result = depth_in + project_out(e_out[col], col)
    for e in (1, 3, 2):
        back_copies[e].wait_recv()
        result = result + project_out(e_in[e], (col + 4 - e) % 4)
    out_ref[...] = result.astype(BF16)

    for ref, i in (
        (look_sib, 0),
        (look_in, 2),
        (look_in, 3),
        (look_in.at[0], 5),
        (part_in.at[0], 7),
        (part_in.at[1], 8),
        (part_in.at[0], 11),
        (part_in.at[1], 12),
        (look_in, 15),
        (c_sib, 17),
        (c_in, 19),
        (d_in.at[pl.ds(0, 3)], 23),
        (e_in.at[pl.ds(0, 3)], 25),
    ):
        settle(ref, sems.at[i])

    @pl.when(row == 0)
    def _():
        settle(d_in.at[pl.ds(0, 4), :, QUAD:], sems.at[21])


def shards(
    x_resid,
    qkv_new,
    kv_cache,
    cache_lens,
    wo_temporal,
    norm_gain,
    w_in,
    embed_rows,
    token_ids,
    depth_gain,
    depth_qkv,
    depth_out,
):
    args = (
        x_resid,
        qkv_new.reshape(ROWS, (GROUP + 2) * HD),
        kv_cache.reshape(ROWS, 2, FRAMES, HD),
        cache_lens,
        wo_temporal,
        norm_gain.reshape(1, COLS),
        w_in.reshape(COLS, DDEP),
        embed_rows.reshape(128, DDEP),
        token_ids.reshape(1, 256),
        depth_gain,
        depth_qkv.reshape(DDEP, 3 * DDEP),
        depth_out.reshape(DDEP, DDEP),
    )
    args = tuple(pltpu.with_memory_space_constraint(a, pltpu.HBM) for a in args)
    dma = pltpu.SemaphoreType.DMA
    vm = pltpu.VMEM
    out = pl.pallas_call(
        frame_kernel,
        name="frame",
        out_shape=jax.ShapeDtypeStruct((ROWS, DDEP), BF16),
        in_specs=[pl.BlockSpec(memory_space=pltpu.HBM)] * len(args),
        out_specs=pl.BlockSpec(memory_space=pltpu.VMEM),
        scratch_shapes=[
            vm((ROWS, FRAMES, HD), BF16),
            vm((ROWS, FRAMES, HD), BF16),
            vm((GROUP * HD, COLS), BF16),
            vm((COLS, DDEP), BF16),
            vm((128, DDEP), BF16),
            vm((DDEP, 3 * DDEP), BF16),
            vm((DDEP, DDEP), BF16),
            vm((32, COLS), BF16),
            vm((ROWS, (GROUP + 2) * HD), BF16),
            pltpu.SMEM((ROWS,), jnp.int32),
            vm((1, COLS), F32),
            vm((1, DDEP), F32),
            vm((1, 256), jnp.int32),
            dma((6,)),
            dma((11,)),
            vm((ROWS * GROUP, HD), F32),
            vm((ROWS * GROUP, HD), F32),
            vm((ROWS * GROUP, HD), F32),
            vm((2, ROWS * HD, HD), BF16),
            vm((HD, HALF_FRAMES), F32),
            vm((ROWS * GROUP, HD), F32),
            vm((2, CHIPS, 2, ROWS, GROUP * HD // 2), BF16),
            vm((2, TP, ROWS, COLS), BF16),
            vm((2, TP - 1, ROWS, COLS), BF16),
            vm((TP, 2, ROWS, COLS), BF16),
            vm((CHIPS, 2, ROWS, 128), BF16),
            vm((CHIPS, ROWS, DDEP), BF16),
            vm((CHIPS, ROWS, DDEP), BF16),
            vm((CHIPS, ROWS, DDEP), BF16),
            vm((CHIPS, ROWS, DDEP), BF16),
            vm((CHIPS - 1, ROWS, DDEP), BF16),
            vm((CHIPS, ROWS, WIDE), BF16),
            vm((CHIPS, ROWS, WIDE), BF16),
            vm((CHIPS, ROWS, WIDE), BF16),
            vm((CHIPS - 1, ROWS, WIDE), BF16),
            vm((4, ROWS, 3 * QUAD), BF16),
            vm((TP, ROWS, 3 * QUAD), BF16),
            vm((4, ROWS, QUAD), BF16),
            vm((4, ROWS, QUAD), BF16),
            dma((14,)),
            dma((30,)),
        ],
        compiler_params=pltpu.CompilerParams(
            collective_id=0, has_side_effects=True, vmem_limit_bytes=40 * 2**20
        ),
        cost_estimate=pl.CostEstimate(flops=10**9, bytes_accessed=19 * 10**6, transcendentals=10**5),
    )(*args)
    return out.reshape(ROWS, 1, DDEP)


def solution(mesh):
    in_specs = (
        P(None, "sess"),
        P("sess", "tp", None),
        P("sess", None, "tp", None, None),
        P("sess"),
        P("tp", "sess"),
        P("sess"),
        P("tp", "sess", None),
        P("tp", "sess", None),
        P(None, "tp"),
        P("tp", None),
        P("tp", None, None),
        P("tp", None, None),
    )
    out_specs = P("sess", "tp", None)
    return jax.shard_map(shards, mesh=mesh, in_specs=in_specs, out_specs=out_specs, check_vma=False)
```

```python
import jax
import jax.numpy as jnp
from jax import lax
from jax.experimental import pallas as pl
from jax.experimental.pallas import tpu as pltpu
from jax.sharding import PartitionSpec as P

MESH = pl.DeviceIdType.MESH
F32 = jnp.float32
BF16 = jnp.bfloat16

D = 8192
EPS = 1e-05
CHIPS = 8
TP = 8
ROWS = 16
GROUP = 8
HD = 128
FRAMES = 1024
COLS = 512
DDEP = 1024
WIDE = DDEP + 128
QUAD = 256
DH = 64
HALF = 8
HALF_FRAMES = FRAMES // 2


def dot(a, b):
    return jnp.dot(a, b, preferred_element_type=F32)


def frame_kernel(
    x_hbm,
    qkv_hbm,
    kv_hbm,
    lens_hbm,
    wo_hbm,
    gain_hbm,
    win_hbm,
    emb_hbm,
    tok_hbm,
    dgain_hbm,
    dqkv_hbm,
    dout_hbm,
    out_ref,
    keys,
    values,
    wo,
    win,
    emb,
    dqkv,
    dout,
    xres,
    qkv,
    lens,
    gain,
    dgain,
    tok,
    kv_sem,
    in_sem,
    q_scr,
    k_scr,
    v_scr,
    query_cols,
    weight_scr,
    o_scr,
    attn_all,
    part,
    part_in,
    hid_all,
    onehot,
    look_own,
    look_sib,
    look_in_sib,
    look_out,
    look_in,
    c_sib,
    c_in_sib,
    c_out,
    c_in,
    d_out,
    d_in,
    e_out,
    e_in,
    direct_sem,
    sems,
):
    s = lax.axis_index("sess")
    t = lax.axis_index("tp")
    chip = s // 2
    core = s % 2
    other = 1 - core
    row = t // 4
    col = t % 4
    sibling = (chip * 2 + other, t)

    def step_of(d):
        return ((0, 0), (0, 1), (0, 3), (1, 0), (0, 2), (1, 1), (1, 3), (1, 2))[d]

    def at(i, d):
        hi, lo = step_of(d)
        return ((i // 4 + hi) % 2) * 4 + (i % 4 + lo) % 4

    def back(i, d):
        hi, lo = step_of(d)
        return ((i // 4 + hi) % 2) * 4 + (i % 4 + 4 - lo) % 4

    far_first = (7, 6, 5, 4, 3, 2, 1)
    near_first = (1, 2, 3, 4, 5, 6, 7)

    def remote(src, dst, send, recv, device):
        return pltpu.make_async_remote_copy(
            src_ref=src,
            dst_ref=dst,
            send_sem=send,
            recv_sem=recv,
            device_id=device,
            device_id_type=MESH,
        )

    def settle(ref, sem):
        pltpu.make_async_copy(ref, ref, sem).wait()

    def load(i, src, dst):
        return pltpu.make_async_copy(src, dst, in_sem.at[i])

    x_load = load(0, x_hbm.at[pl.ds(pl.multiple_of(t * 32, 32), 32)], xres)
    qkv_load = load(1, qkv_hbm, qkv)
    lens_load = load(2, lens_hbm, lens)
    gain_load = load(3, gain_hbm, gain)
    dgain_load = load(4, dgain_hbm, dgain)
    tok_load = load(5, tok_hbm, tok)
    emb_load = load(6, emb_hbm, emb)
    wo_load = load(7, wo_hbm, wo)
    win_load = load(8, win_hbm, win)
    dqkv_load = load(9, dqkv_hbm, dqkv)
    dout_load = load(10, dout_hbm, dout)
    def cache_load(which, first, count, dst, i):
        part_of = pl.ds(first, count)
        return pltpu.make_async_copy(kv_hbm.at[part_of, which], dst.at[part_of], kv_sem.at[i])

    key_loads = [cache_load(0, a * HALF, HALF, keys, a) for a in range(2)]
    value_loads = [cache_load(1, g * 4, 4, values, 2 + g) for g in range(4)]
    loads = [qkv_load, key_loads[0], lens_load, value_loads[0], value_loads[1], key_loads[1], value_loads[2], value_loads[3]]
    for copy in loads:
        copy.start()

    barrier = pltpu.get_barrier_semaphore()
    pl.semaphore_signal(barrier, inc=1, device_id=sibling, device_id_type=MESH)
    for d in far_first:
        for device in ((at(chip, d) * 2, t), (at(chip, d) * 2 + 1, t), (s, at(t, d))):
            pl.semaphore_signal(barrier, inc=1, device_id=device, device_id_type=MESH)
    for copy in (tok_load, emb_load, gain_load, dgain_load, x_load):
        copy.start()

    qkv_load.wait()
    new_keys = qkv[:, GROUP * HD : (GROUP + 1) * HD].astype(F32)
    new_values = qkv[:, (GROUP + 1) * HD :].astype(F32)
    for h in range(GROUP):
        rows_h = pl.ds(h, ROWS, stride=GROUP)
        q_scr[rows_h, :] = qkv[:, h * HD : (h + 1) * HD].astype(F32)
        k_scr[rows_h, :] = new_keys
        v_scr[rows_h, :] = new_values
    query_t = q_scr[...].T
    scale = HD ** (-0.5)
    new_score = jnp.sum(query_t * k_scr[...].T, axis=0, keepdims=True) * scale
    new_score = jnp.broadcast_to(new_score, (8, HD))
    column = lax.broadcasted_iota(jnp.int32, (HD, HD), 1)
    line = lax.broadcasted_iota(jnp.int32, (8, HD), 1)
    swapped = pltpu.roll(query_t, 64, 1)
    swapped_score = pltpu.roll(new_score, 64, 1)
    lens_load.wait()
    half_scores = []
    lives = []
    for a in range(2):
        half_query = jnp.where((column < 64) == (a == 0), query_t, swapped)
        half_scores.append(jnp.where((line < 64) == (a == 0), new_score, swapped_score))
        live = jnp.zeros((8, HD), jnp.int32)
        for i in range(HALF):
            live = jnp.where((line // GROUP) % HALF == i, lens[a * HALF + i], live)
            for f in range(2):
                block = f * HALF + i
                query_cols[a, block * HD : (block + 1) * HD, :] = jnp.where(
                    column // GROUP == block, half_query, 0.0
                ).astype(BF16)
        lives.append(live - jnp.where(line < 64, 0, HALF_FRAMES))
    frame = lax.broadcasted_iota(jnp.int32, (HALF_FRAMES, HD), 0)

    def attend_half(a):
        key_loads[a].wait()
        joined = jnp.concatenate(
            [
                keys[a * HALF + i, f * HALF_FRAMES : (f + 1) * HALF_FRAMES]
                for f in range(2)
                for i in range(HALF)
            ],
            axis=1,
        )
        scores = dot(joined, query_cols[a]) * scale
        masked = jnp.where(frame < lives[a][:1], scores, -1e30)
        top = jnp.broadcast_to(jnp.max(masked, axis=0, keepdims=True), (8, HD))
        peak = jnp.maximum(jnp.maximum(top, pltpu.roll(top, 64, 1)), half_scores[a])
        expo = jnp.exp(masked - peak[:1])
        new_expo = jnp.exp(half_scores[a] - peak)
        total = jnp.broadcast_to(jnp.sum(expo, axis=0, keepdims=True), (8, HD))
        inv = 1.0 / (total + pltpu.roll(total, 64, 1) + new_expo)
        weight_scr[...] = (expo * inv[:1]).T
        new_weight = (new_expo * inv).astype(BF16).astype(F32)
        new_column = jnp.broadcast_to(new_weight[:1], (HD, HD)).T
        for g in range(2):
            value_loads[a * 2 + g].wait()
            for i in range(g * 4, g * 4 + 4, 2):
                session = a * HALF + i
                context = None
                for f in range(2):
                    rows_f = slice(f * 64 + i * GROUP, f * 64 + (i + 2) * GROUP)
                    frames = slice(f * HALF_FRAMES, (f + 1) * HALF_FRAMES)
                    pair = jnp.concatenate([values[session, frames], values[session + 1, frames]], axis=1)
                    partial = dot(weight_scr[rows_f, :].astype(BF16), pair)
                    context = partial if f == 0 else context + partial
                rows_i = slice(i * GROUP, (i + 2) * GROUP)
                rows_s = slice(session * GROUP, (session + 2) * GROUP)
                own = jnp.concatenate([context[:GROUP, :HD], context[GROUP:, HD:]], axis=0)
                o_scr[rows_s, :] = own + new_column[rows_i] * v_scr[rows_s, :]

    gather = {}

    def gather_half(a):
        for h in range(4):
            low_heads = o_scr[pl.ds(a * 64 + h, HALF, stride=GROUP), :]
            high_heads = o_scr[pl.ds(a * 64 + h + 4, HALF, stride=GROUP), :]
            attn_all[a, chip, core, :, h * HD : (h + 1) * HD] = jnp.concatenate(
                [low_heads, high_heads], axis=0
            ).astype(BF16)
        mine = attn_all.at[a, chip, core]
        if a == 0:
            pl.semaphore_wait(barrier, 22)
        for d in far_first:
            gather[a, d] = remote(
                mine, mine, sems.at[2], direct_sem.at[a * 7 + d - 1], (at(chip, d) * 2 + other, t)
            )
            gather[a, d].start()
        remote(mine, mine, sems.at[5], sems.at[6], sibling).start()

    attend_half(0)
    gather_half(0)
    wo_load.start()
    win_load.start()
    attend_half(1)
    gather_half(1)
    dqkv_load.start()
    dout_load.start()

    tok_load.wait()
    emb_load.wait()
    entry = lax.broadcasted_iota(jnp.int32, (128, 256), 0) + s * 128
    hot = jnp.where(tok[...] == entry, 1.0, 0.0).T.astype(BF16)
    onehot[...] = hot.reshape(CHIPS, 2, ROWS, 128)

    def look(parity):
        rows = onehot[:, pl.ds(parity, 1)].reshape(CHIPS * ROWS, 128)
        return dot(rows, emb[...]).astype(BF16).reshape(CHIPS, ROWS, DDEP)

    look_sib[...] = look(other)
    look_to_sib = remote(look_sib, look_in_sib, sems.at[0], sems.at[1], sibling)
    look_to_sib.start()
    look_own[...] = look(core)

    gain_load.wait()
    win_load.wait()
    gain_col = jnp.broadcast_to(gain[...], (128, COLS)).T
    for j in range(DDEP // 128):
        cols = slice(j * 128, (j + 1) * 128)
        win[:, cols] = (win[:, cols].astype(F32) * gain_col).astype(BF16)

    for a in range(2):
        for d in near_first:
            gather[a, d].wait_recv()
            block = attn_all.at[a, back(chip, d), other]
            remote(block, block, sems.at[3], sems.at[4], sibling).start()
    settle(look_in.at[0], sems.at[6])
    wo_load.wait()

    def attention_rows(parity, chips):
        blocks = []
        for i in chips:
            for a in range(2):
                block = attn_all[a, i, parity].astype(F32)
                blocks.append(jnp.concatenate([block[:HALF], block[HALF:]], axis=1))
        return jnp.concatenate(blocks, axis=0).astype(BF16)

    def reduce_start(half, parity):
        for offsets in ((7, 6, 5, 4), (3, 2, 1, 0)):
            rows = attention_rows(parity, [at(t, d) for d in offsets])
            product = dot(rows, wo[...]).astype(BF16).reshape(4, ROWS, COLS)
            for i, d in enumerate(offsets):
                part[half, d] = product[i]
                if d:
                    remote(
                        part.at[half, d], part_in.at[half, d - 1], sems.at[7 + half], sems.at[9 + half], (s, at(t, d))
                    ).start()

    reduce_start(0, other)
    settle(look_in, sems.at[4])
    reduce_start(1, core)
    x_load.wait()

    def gather_start(half, parity):
        hidden = xres[pl.ds(pl.multiple_of(parity * ROWS, ROWS), ROWS)].astype(F32) + part[half, 0].astype(F32)
        settle(part_in.at[half], sems.at[9 + half])
        for d in range(CHIPS - 1):
            hidden = hidden + part_in[half, d].astype(F32)
        hid_all[t, parity] = hidden.astype(BF16)
        block = hid_all.at[t, parity]
        for d in far_first:
            remote(block, block, sems.at[11 + half], sems.at[13 + half], (s, at(t, d))).start()

    gather_start(0, other)
    gather_start(1, core)
    look_to_sib.wait_recv()
    look_out[...] = (look_own[...].astype(F32) + look_in_sib[...].astype(F32)).astype(BF16)
    for d in far_first:
        to = at(chip, d)
        remote(look_out.at[to], look_in.at[d - 1], sems.at[15], sems.at[16], (to * 2 + core, t)).start()

    lane = lax.broadcasted_iota(jnp.int32, (4 * ROWS, 128), 1)

    def project(parity, blocks):
        rows = jnp.concatenate([hid_all[i, parity] for i in blocks], axis=0)
        wide = rows.astype(F32)
        squares = jnp.sum(wide * wide, axis=1, keepdims=True)
        high = squares.astype(BF16).astype(F32)
        low = squares - high
        extra = jnp.where(lane == 2 * core, high, 0.0) + jnp.where(lane == 2 * core + 1, low, 0.0)
        return dot(rows, win[...]).reshape(len(blocks), ROWS, DDEP), extra.reshape(len(blocks), ROWS, 128)

    settle(part_in.at[0], sems.at[13])
    to_sib = {}
    for k, offsets in enumerate(((7, 6, 5, 4), (3, 2, 1, 0))):
        product, extra = project(other, [at(chip, d) for d in offsets])
        for i, d in enumerate(offsets):
            c_sib[d, :, :DDEP] = product[i].astype(BF16)
            c_sib[d, :, DDEP:] = extra[i].astype(BF16)
        part_of = pl.ds(offsets[3], 4)
        to_sib[k] = remote(
            c_sib.at[part_of], c_in_sib.at[part_of], sems.at[17], sems.at[18 if k == 0 else 27], sibling
        )
        to_sib[k].start()
    settle(part_in.at[1], sems.at[14])
    for k, offsets in enumerate(((7, 6, 5, 4), (3, 2, 1, 0))):
        product, extra = project(core, [at(chip, d) for d in offsets])
        to_sib[k].wait_recv()
        for i, d in enumerate(offsets):
            to = at(chip, d)
            c_out[d, :, :DDEP] = (product[i] + c_in_sib[d, :, :DDEP].astype(F32)).astype(BF16)
            c_out[d, :, DDEP:] = (extra[i] + c_in_sib[d, :, DDEP:].astype(F32)).astype(BF16)
            if d:
                remote(c_out.at[d], c_in.at[d - 1], sems.at[19], sems.at[20], (to * 2 + core, t)).start()
    settle(look_in, sems.at[16])
    looked = look_out[chip].astype(F32)
    for d in range(CHIPS - 1):
        looked = looked + look_in[d].astype(F32)
    summed = c_out[0].astype(F32)
    settle(c_in, sems.at[20])
    for d in range(CHIPS - 1):
        summed = summed + c_in[d].astype(F32)
    squares = jnp.sum(summed[:, DDEP:], axis=1, keepdims=True)
    depth_in = summed[:, :DDEP] * lax.rsqrt(squares / D + EPS) + looked

    dgain_load.wait()
    mean_sq = jnp.mean(depth_in * depth_in, axis=1, keepdims=True)
    normed = (depth_in * lax.rsqrt(mean_sq + EPS) * dgain[...]).astype(BF16)
    dqkv_load.wait()
    for e in (2, 1, 3, 0):
        to = (col + e) % 4
        for p in range(3):
            first = pl.multiple_of(p * DDEP + to * QUAD, QUAD)
            d_out[e, :, p * QUAD : (p + 1) * QUAD] = dot(normed, dqkv[:, pl.ds(first, QUAD)]).astype(BF16)

        @pl.when(row == 0)
        def _(e=e, to=to):
            remote(
                d_out.at[e, :, QUAD:], d_in.at[t, :, QUAD:], sems.at[21], sems.at[22], (s, 4 + to)
            ).start()

        if e:
            remote(d_out.at[e], d_in.at[t], sems.at[23], sems.at[24], (s, row * 4 + to)).start()
    d_in[t] = d_out[0]
    settle(d_in.at[pl.ds(0, 3)], sems.at[24])

    head_r = lax.broadcasted_iota(jnp.int32, (QUAD, QUAD), 0) // DH
    head_c = lax.broadcasted_iota(jnp.int32, (QUAD, QUAD), 1) // DH
    same_head = jnp.where(head_r == head_c, 1.0, 0.0).astype(BF16)

    def attend(codebooks):
        count = codebooks[-1] + 1
        qs = [d_in[c, :, :QUAD].astype(F32) for c in codebooks]
        ks = [d_in[c, :, QUAD : 2 * QUAD].astype(F32) for c in range(count)]
        vs = [d_in[c, :, 2 * QUAD :].astype(F32) for c in range(count)]
        products = jnp.concatenate(
            [qs[i] * ks[j] for i, c in enumerate(codebooks) for j in range(c + 1)], axis=0
        )
        high = products.astype(BF16)
        low = (products - high.astype(F32)).astype(BF16)
        scores = (dot(high, same_head) + dot(low, same_head)) * DH ** (-0.5)
        start = 0
        for i, c in enumerate(codebooks):
            lines = [scores[(start + j) * ROWS : (start + j + 1) * ROWS] for j in range(c + 1)]
            start += c + 1
            top = lines[0]
            for line in lines[1:]:
                top = jnp.maximum(top, line)
            total = jnp.zeros((ROWS, QUAD), F32)
            context = jnp.zeros((ROWS, QUAD), F32)
            for j, line in enumerate(lines):
                weight = jnp.exp(line - top)
                total = total + weight
                context = context + weight * vs[j]
            e_out[i] = (context / total).astype(BF16)

    @pl.when(row == 0)
    def _():
        attend((0, 1, 2, 3))

    @pl.when(row == 1)
    def _():
        settle(d_in.at[pl.ds(0, 4), :, QUAD:], sems.at[22])
        attend((4, 5, 6, 7))

    back_copies = {}
    for k, e in enumerate((2, 1, 3)):
        to = (col + e) % 4
        back_copies[e] = remote(e_out.at[to], e_in.at[e], sems.at[25], sems.at[(26, 28, 29)[k]], (s, row * 4 + to))
        back_copies[e].start()

    def project_out(block, source):
        first = pl.multiple_of(source * QUAD, QUAD)
        return dot(block, dout[pl.ds(first, QUAD), :])

    dout_load.wait()
    result = depth_in + project_out(e_out[col], col)
    for e in (1, 3, 2):
        back_copies[e].wait_recv()
        result = result + project_out(e_in[e], (col + 4 - e) % 4)
    out_ref[...] = result.astype(BF16)

    for ref, i in (
        (look_sib, 0),
        (look_in, 2),
        (look_in, 3),
        (look_in.at[0], 5),
        (part_in.at[0], 7),
        (part_in.at[1], 8),
        (part_in.at[0], 11),
        (part_in.at[1], 12),
        (look_in, 15),
        (c_sib, 17),
        (c_in, 19),
        (d_in.at[pl.ds(0, 3)], 23),
        (e_in.at[pl.ds(0, 3)], 25),
    ):
        settle(ref, sems.at[i])

    @pl.when(row == 0)
    def _():
        settle(d_in.at[pl.ds(0, 4), :, QUAD:], sems.at[21])


def shards(
    x_resid,
    qkv_new,
    kv_cache,
    cache_lens,
    wo_temporal,
    norm_gain,
    w_in,
    embed_rows,
    token_ids,
    depth_gain,
    depth_qkv,
    depth_out,
):
    args = (
        x_resid,
        qkv_new.reshape(ROWS, (GROUP + 2) * HD),
        kv_cache.reshape(ROWS, 2, FRAMES, HD),
        cache_lens,
        wo_temporal,
        norm_gain.reshape(1, COLS),
        w_in.reshape(COLS, DDEP),
        embed_rows.reshape(128, DDEP),
        token_ids.reshape(1, 256),
        depth_gain,
        depth_qkv.reshape(DDEP, 3 * DDEP),
        depth_out.reshape(DDEP, DDEP),
    )
    args = tuple(pltpu.with_memory_space_constraint(a, pltpu.HBM) for a in args)
    dma = pltpu.SemaphoreType.DMA
    vm = pltpu.VMEM
    out = pl.pallas_call(
        frame_kernel,
        name="frame",
        out_shape=jax.ShapeDtypeStruct((ROWS, DDEP), BF16),
        in_specs=[pl.BlockSpec(memory_space=pltpu.HBM)] * len(args),
        out_specs=pl.BlockSpec(memory_space=pltpu.VMEM),
        scratch_shapes=[
            vm((ROWS, FRAMES, HD), BF16),
            vm((ROWS, FRAMES, HD), BF16),
            vm((GROUP * HD, COLS), BF16),
            vm((COLS, DDEP), BF16),
            vm((128, DDEP), BF16),
            vm((DDEP, 3 * DDEP), BF16),
            vm((DDEP, DDEP), BF16),
            vm((32, COLS), BF16),
            vm((ROWS, (GROUP + 2) * HD), BF16),
            pltpu.SMEM((ROWS,), jnp.int32),
            vm((1, COLS), F32),
            vm((1, DDEP), F32),
            vm((1, 256), jnp.int32),
            dma((6,)),
            dma((11,)),
            vm((ROWS * GROUP, HD), F32),
            vm((ROWS * GROUP, HD), F32),
            vm((ROWS * GROUP, HD), F32),
            vm((2, ROWS * HD, HD), BF16),
            vm((HD, HALF_FRAMES), F32),
            vm((ROWS * GROUP, HD), F32),
            vm((2, CHIPS, 2, ROWS, GROUP * HD // 2), BF16),
            vm((2, TP, ROWS, COLS), BF16),
            vm((2, TP - 1, ROWS, COLS), BF16),
            vm((TP, 2, ROWS, COLS), BF16),
            vm((CHIPS, 2, ROWS, 128), BF16),
            vm((CHIPS, ROWS, DDEP), BF16),
            vm((CHIPS, ROWS, DDEP), BF16),
            vm((CHIPS, ROWS, DDEP), BF16),
            vm((CHIPS, ROWS, DDEP), BF16),
            vm((CHIPS - 1, ROWS, DDEP), BF16),
            vm((CHIPS, ROWS, WIDE), BF16),
            vm((CHIPS, ROWS, WIDE), BF16),
            vm((CHIPS, ROWS, WIDE), BF16),
            vm((CHIPS - 1, ROWS, WIDE), BF16),
            vm((4, ROWS, 3 * QUAD), BF16),
            vm((TP, ROWS, 3 * QUAD), BF16),
            vm((4, ROWS, QUAD), BF16),
            vm((4, ROWS, QUAD), BF16),
            dma((14,)),
            dma((30,)),
        ],
        compiler_params=pltpu.CompilerParams(
            collective_id=0, has_side_effects=True, vmem_limit_bytes=40 * 2**20
        ),
        cost_estimate=pl.CostEstimate(flops=10**9, bytes_accessed=19 * 10**6, transcendentals=10**5),
    )(*args)
    return out.reshape(ROWS, 1, DDEP)


def solution(mesh):
    in_specs = (
        P(None, "sess"),
        P("sess", "tp", None),
        P("sess", None, "tp", None, None),
        P("sess"),
        P("tp", "sess"),
        P("sess"),
        P("tp", "sess", None),
        P("tp", "sess", None),
        P(None, "tp"),
        P("tp", None),
        P("tp", None, None),
        P("tp", None, None),
    )
    out_specs = P("sess", "tp", None)
    return jax.shard_map(shards, mesh=mesh, in_specs=in_specs, out_specs=out_specs, check_vma=False)
```

```python
import jax
import jax.numpy as jnp
from jax import lax
from jax.experimental import pallas as pl
from jax.experimental.pallas import tpu as pltpu
from jax.sharding import PartitionSpec as P

MESH = pl.DeviceIdType.MESH
F32 = jnp.float32
BF16 = jnp.bfloat16

D = 8192
EPS = 1e-05
CHIPS = 8
TP = 8
ROWS = 16
GROUP = 8
HD = 128
FRAMES = 1024
COLS = 512
DDEP = 1024
WIDE = DDEP + 128
QUAD = 256
DH = 64
HALF = 8
HALF_FRAMES = FRAMES // 2


def dot(a, b):
    return jnp.dot(a, b, preferred_element_type=F32)


def frame_kernel(
    x_hbm,
    qkv_hbm,
    kv_hbm,
    lens_hbm,
    wo_hbm,
    gain_hbm,
    win_hbm,
    emb_hbm,
    tok_hbm,
    dgain_hbm,
    dqkv_hbm,
    dout_hbm,
    out_ref,
    keys,
    values,
    wo,
    win,
    emb,
    dqkv,
    dout,
    xres,
    qkv,
    lens,
    gain,
    dgain,
    tok,
    kv_sem,
    in_sem,
    q_scr,
    k_scr,
    v_scr,
    query_cols,
    weight_scr,
    o_scr,
    attn_all,
    part,
    part_in,
    hid_all,
    onehot,
    look_own,
    look_sib,
    look_in_sib,
    look_out,
    look_in,
    c_sib,
    c_in_sib,
    c_out,
    c_in,
    d_out,
    d_in,
    e_out,
    e_in,
    direct_sem,
    sems,
):
    s = lax.axis_index("sess")
    t = lax.axis_index("tp")
    chip = s // 2
    core = s % 2
    other = 1 - core
    row = t // 4
    col = t % 4
    sibling = (chip * 2 + other, t)

    def step_of(d):
        return ((0, 0), (0, 1), (0, 3), (0, 2), (1, 0), (1, 1), (1, 3), (1, 2))[d]

    def at(i, d):
        hi, lo = step_of(d)
        return ((i // 4 + hi) % 2) * 4 + (i % 4 + lo) % 4

    def back(i, d):
        hi, lo = step_of(d)
        return ((i // 4 + hi) % 2) * 4 + (i % 4 + 4 - lo) % 4

    far_first = (7, 6, 5, 4, 3, 2, 1)
    near_first = (1, 2, 3, 4, 5, 6, 7)

    def remote(src, dst, send, recv, device):
        return pltpu.make_async_remote_copy(
            src_ref=src,
            dst_ref=dst,
            send_sem=send,
            recv_sem=recv,
            device_id=device,
            device_id_type=MESH,
        )

    def settle(ref, sem):
        pltpu.make_async_copy(ref, ref, sem).wait()

    def load(i, src, dst):
        return pltpu.make_async_copy(src, dst, in_sem.at[i])

    x_load = load(0, x_hbm.at[pl.ds(pl.multiple_of(t * 32, 32), 32)], xres)
    qkv_load = load(1, qkv_hbm, qkv)
    lens_load = load(2, lens_hbm, lens)
    gain_load = load(3, gain_hbm, gain)
    dgain_load = load(4, dgain_hbm, dgain)
    tok_load = load(5, tok_hbm, tok)
    emb_load = load(6, emb_hbm, emb)
    wo_load = load(7, wo_hbm, wo)
    win_load = load(8, win_hbm, win)
    dqkv_load = load(9, dqkv_hbm, dqkv)
    dout_load = load(10, dout_hbm, dout)
    def cache_load(which, first, count, dst, i):
        part_of = pl.ds(first, count)
        return pltpu.make_async_copy(kv_hbm.at[part_of, which], dst.at[part_of], kv_sem.at[i])

    key_loads = [cache_load(0, a * HALF, HALF, keys, a) for a in range(2)]
    value_loads = [cache_load(1, g * 4, 4, values, 2 + g) for g in range(4)]
    loads = [qkv_load, key_loads[0], lens_load, value_loads[0], value_loads[1], key_loads[1], value_loads[2], value_loads[3]]
    for copy in loads:
        copy.start()

    barrier = pltpu.get_barrier_semaphore()
    pl.semaphore_signal(barrier, inc=1, device_id=sibling, device_id_type=MESH)
    for d in far_first:
        for device in ((at(chip, d) * 2, t), (at(chip, d) * 2 + 1, t), (s, at(t, d))):
            pl.semaphore_signal(barrier, inc=1, device_id=device, device_id_type=MESH)
    for copy in (tok_load, emb_load, gain_load, dgain_load, x_load):
        copy.start()

    qkv_load.wait()
    new_keys = qkv[:, GROUP * HD : (GROUP + 1) * HD].astype(F32)
    new_values = qkv[:, (GROUP + 1) * HD :].astype(F32)
    for h in range(GROUP):
        rows_h = pl.ds(h, ROWS, stride=GROUP)
        q_scr[rows_h, :] = qkv[:, h * HD : (h + 1) * HD].astype(F32)
        k_scr[rows_h, :] = new_keys
        v_scr[rows_h, :] = new_values
    query_t = q_scr[...].T
    scale = HD ** (-0.5)
    new_score = jnp.sum(query_t * k_scr[...].T, axis=0, keepdims=True) * scale
    new_score = jnp.broadcast_to(new_score, (8, HD))
    column = lax.broadcasted_iota(jnp.int32, (HD, HD), 1)
    line = lax.broadcasted_iota(jnp.int32, (8, HD), 1)
    swapped = pltpu.roll(query_t, 64, 1)
    swapped_score = pltpu.roll(new_score, 64, 1)
    lens_load.wait()
    half_scores = []
    lives = []
    for a in range(2):
        half_query = jnp.where((column < 64) == (a == 0), query_t, swapped)
        half_scores.append(jnp.where((line < 64) == (a == 0), new_score, swapped_score))
        live = jnp.zeros((8, HD), jnp.int32)
        for i in range(HALF):
            live = jnp.where((line // GROUP) % HALF == i, lens[a * HALF + i], live)
            for f in range(2):
                block = f * HALF + i
                query_cols[a, block * HD : (block + 1) * HD, :] = jnp.where(
                    column // GROUP == block, half_query, 0.0
                ).astype(BF16)
        lives.append(live - jnp.where(line < 64, 0, HALF_FRAMES))
    frame = lax.broadcasted_iota(jnp.int32, (HALF_FRAMES, HD), 0)

    def attend_half(a):
        key_loads[a].wait()
        joined = jnp.concatenate(
            [
                keys[a * HALF + i, f * HALF_FRAMES : (f + 1) * HALF_FRAMES]
                for f in range(2)
                for i in range(HALF)
            ],
            axis=1,
        )
        scores = dot(joined, query_cols[a]) * scale
        masked = jnp.where(frame < lives[a][:1], scores, -1e30)
        top = jnp.broadcast_to(jnp.max(masked, axis=0, keepdims=True), (8, HD))
        peak = jnp.maximum(jnp.maximum(top, pltpu.roll(top, 64, 1)), half_scores[a])
        expo = jnp.exp(masked - peak[:1])
        new_expo = jnp.exp(half_scores[a] - peak)
        total = jnp.broadcast_to(jnp.sum(expo, axis=0, keepdims=True), (8, HD))
        inv = 1.0 / (total + pltpu.roll(total, 64, 1) + new_expo)
        weight_scr[...] = (expo * inv[:1]).T
        new_weight = (new_expo * inv).astype(BF16).astype(F32)
        new_column = jnp.broadcast_to(new_weight[:1], (HD, HD)).T
        for g in range(2):
            value_loads[a * 2 + g].wait()
            for i in range(g * 4, g * 4 + 4, 2):
                session = a * HALF + i
                context = None
                for f in range(2):
                    rows_f = slice(f * 64 + i * GROUP, f * 64 + (i + 2) * GROUP)
                    frames = slice(f * HALF_FRAMES, (f + 1) * HALF_FRAMES)
                    pair = jnp.concatenate([values[session, frames], values[session + 1, frames]], axis=1)
                    partial = dot(weight_scr[rows_f, :].astype(BF16), pair)
                    context = partial if f == 0 else context + partial
                rows_i = slice(i * GROUP, (i + 2) * GROUP)
                rows_s = slice(session * GROUP, (session + 2) * GROUP)
                own = jnp.concatenate([context[:GROUP, :HD], context[GROUP:, HD:]], axis=0)
                o_scr[rows_s, :] = own + new_column[rows_i] * v_scr[rows_s, :]

    gather = {}

    def gather_half(a):
        for h in range(4):
            low_heads = o_scr[pl.ds(a * 64 + h, HALF, stride=GROUP), :]
            high_heads = o_scr[pl.ds(a * 64 + h + 4, HALF, stride=GROUP), :]
            attn_all[a, chip, core, :, h * HD : (h + 1) * HD] = jnp.concatenate(
                [low_heads, high_heads], axis=0
            ).astype(BF16)
        mine = attn_all.at[a, chip, core]
        if a == 0:
            pl.semaphore_wait(barrier, 22)
        for d in far_first:
            gather[a, d] = remote(
                mine, mine, sems.at[2], direct_sem.at[a * 7 + d - 1], (at(chip, d) * 2 + other, t)
            )
            gather[a, d].start()
        remote(mine, mine, sems.at[5], sems.at[6], sibling).start()

    attend_half(0)
    gather_half(0)
    wo_load.start()
    win_load.start()
    attend_half(1)
    gather_half(1)
    dqkv_load.start()
    dout_load.start()

    tok_load.wait()
    emb_load.wait()
    entry = lax.broadcasted_iota(jnp.int32, (128, 256), 0) + s * 128
    hot = jnp.where(tok[...] == entry, 1.0, 0.0).T.astype(BF16)
    onehot[...] = hot.reshape(CHIPS, 2, ROWS, 128)

    def look(parity):
        rows = onehot[:, pl.ds(parity, 1)].reshape(CHIPS * ROWS, 128)
        return dot(rows, emb[...]).astype(BF16).reshape(CHIPS, ROWS, DDEP)

    look_sib[...] = look(other)
    look_to_sib = remote(look_sib, look_in_sib, sems.at[0], sems.at[1], sibling)
    look_to_sib.start()
    look_own[...] = look(core)

    gain_load.wait()
    win_load.wait()
    gain_col = jnp.broadcast_to(gain[...], (128, COLS)).T
    for j in range(DDEP // 128):
        cols = slice(j * 128, (j + 1) * 128)
        win[:, cols] = (win[:, cols].astype(F32) * gain_col).astype(BF16)

    for a in range(2):
        for d in near_first:
            gather[a, d].wait_recv()
            block = attn_all.at[a, back(chip, d), other]
            remote(block, block, sems.at[3], sems.at[4], sibling).start()
    settle(look_in.at[0], sems.at[6])
    wo_load.wait()

    def attention_rows(parity, chips):
        blocks = []
        for i in chips:
            for a in range(2):
                block = attn_all[a, i, parity].astype(F32)
                blocks.append(jnp.concatenate([block[:HALF], block[HALF:]], axis=1))
        return jnp.concatenate(blocks, axis=0).astype(BF16)

    def reduce_start(half, parity):
        for offsets in ((7, 6, 5, 4), (3, 2, 1, 0)):
            rows = attention_rows(parity, [at(t, d) for d in offsets])
            product = dot(rows, wo[...]).astype(BF16).reshape(4, ROWS, COLS)
            for i, d in enumerate(offsets):
                part[half, d] = product[i]
                if d:
                    remote(
                        part.at[half, d], part_in.at[half, d - 1], sems.at[7 + half], sems.at[9 + half], (s, at(t, d))
                    ).start()

    reduce_start(0, other)
    settle(look_in, sems.at[4])
    reduce_start(1, core)
    x_load.wait()

    def gather_start(half, parity):
        hidden = xres[pl.ds(pl.multiple_of(parity * ROWS, ROWS), ROWS)].astype(F32) + part[half, 0].astype(F32)
        settle(part_in.at[half], sems.at[9 + half])
        for d in range(CHIPS - 1):
            hidden = hidden + part_in[half, d].astype(F32)
        hid_all[t, parity] = hidden.astype(BF16)
        block = hid_all.at[t, parity]
        for d in far_first:
            remote(block, block, sems.at[11 + half], sems.at[13 + half], (s, at(t, d))).start()

    gather_start(0, other)
    gather_start(1, core)
    look_to_sib.wait_recv()
    look_out[...] = (look_own[...].astype(F32) + look_in_sib[...].astype(F32)).astype(BF16)
    for d in far_first:
        to = at(chip, d)
        remote(look_out.at[to], look_in.at[d - 1], sems.at[15], sems.at[16], (to * 2 + core, t)).start()

    lane = lax.broadcasted_iota(jnp.int32, (4 * ROWS, 128), 1)

    def project(parity, blocks):
        rows = jnp.concatenate([hid_all[i, parity] for i in blocks], axis=0)
        wide = rows.astype(F32)
        squares = jnp.sum(wide * wide, axis=1, keepdims=True)
        high = squares.astype(BF16).astype(F32)
        low = squares - high
        extra = jnp.where(lane == 2 * core, high, 0.0) + jnp.where(lane == 2 * core + 1, low, 0.0)
        return dot(rows, win[...]).reshape(len(blocks), ROWS, DDEP), extra.reshape(len(blocks), ROWS, 128)

    settle(part_in.at[0], sems.at[13])
    to_sib = {}
    for k, offsets in enumerate(((7, 6, 5, 4), (3, 2, 1, 0))):
        product, extra = project(other, [at(chip, d) for d in offsets])
        for i, d in enumerate(offsets):
            c_sib[d, :, :DDEP] = product[i].astype(BF16)
            c_sib[d, :, DDEP:] = extra[i].astype(BF16)
        part_of = pl.ds(offsets[3], 4)
        to_sib[k] = remote(
            c_sib.at[part_of], c_in_sib.at[part_of], sems.at[17], sems.at[18 if k == 0 else 27], sibling
        )
        to_sib[k].start()
    settle(part_in.at[1], sems.at[14])
    for k, offsets in enumerate(((7, 6, 5, 4), (3, 2, 1, 0))):
        product, extra = project(core, [at(chip, d) for d in offsets])
        to_sib[k].wait_recv()
        for i, d in enumerate(offsets):
            to = at(chip, d)
            c_out[d, :, :DDEP] = (product[i] + c_in_sib[d, :, :DDEP].astype(F32)).astype(BF16)
            c_out[d, :, DDEP:] = (extra[i] + c_in_sib[d, :, DDEP:].astype(F32)).astype(BF16)
            if d:
                remote(c_out.at[d], c_in.at[d - 1], sems.at[19], sems.at[20], (to * 2 + core, t)).start()
    settle(look_in, sems.at[16])
    looked = look_out[chip].astype(F32)
    for d in range(CHIPS - 1):
        looked = looked + look_in[d].astype(F32)
    summed = c_out[0].astype(F32)
    settle(c_in, sems.at[20])
    for d in range(CHIPS - 1):
        summed = summed + c_in[d].astype(F32)
    squares = jnp.sum(summed[:, DDEP:], axis=1, keepdims=True)
    depth_in = summed[:, :DDEP] * lax.rsqrt(squares / D + EPS) + looked

    dgain_load.wait()
    mean_sq = jnp.mean(depth_in * depth_in, axis=1, keepdims=True)
    normed = (depth_in * lax.rsqrt(mean_sq + EPS) * dgain[...]).astype(BF16)
    dqkv_load.wait()
    for e in (2, 1, 3, 0):
        to = (col + e) % 4
        for p in range(3):
            first = pl.multiple_of(p * DDEP + to * QUAD, QUAD)
            d_out[e, :, p * QUAD : (p + 1) * QUAD] = dot(normed, dqkv[:, pl.ds(first, QUAD)]).astype(BF16)

        @pl.when(row == 0)
        def _(e=e, to=to):
            remote(
                d_out.at[e, :, QUAD:], d_in.at[t, :, QUAD:], sems.at[21], sems.at[22], (s, 4 + to)
            ).start()

        if e:
            remote(d_out.at[e], d_in.at[t], sems.at[23], sems.at[24], (s, row * 4 + to)).start()
    d_in[t] = d_out[0]
    settle(d_in.at[pl.ds(0, 3)], sems.at[24])

    head_r = lax.broadcasted_iota(jnp.int32, (QUAD, QUAD), 0) // DH
    head_c = lax.broadcasted_iota(jnp.int32, (QUAD, QUAD), 1) // DH
    same_head = jnp.where(head_r == head_c, 1.0, 0.0).astype(BF16)

    def attend(codebooks):
        count = codebooks[-1] + 1
        qs = [d_in[c, :, :QUAD].astype(F32) for c in codebooks]
        ks = [d_in[c, :, QUAD : 2 * QUAD].astype(F32) for c in range(count)]
        vs = [d_in[c, :, 2 * QUAD :].astype(F32) for c in range(count)]
        products = jnp.concatenate(
            [qs[i] * ks[j] for i, c in enumerate(codebooks) for j in range(c + 1)], axis=0
        )
        high = products.astype(BF16)
        low = (products - high.astype(F32)).astype(BF16)
        scores = (dot(high, same_head) + dot(low, same_head)) * DH ** (-0.5)
        start = 0
        for i, c in enumerate(codebooks):
            lines = [scores[(start + j) * ROWS : (start + j + 1) * ROWS] for j in range(c + 1)]
            start += c + 1
            top = lines[0]
            for line in lines[1:]:
                top = jnp.maximum(top, line)
            total = jnp.zeros((ROWS, QUAD), F32)
            context = jnp.zeros((ROWS, QUAD), F32)
            for j, line in enumerate(lines):
                weight = jnp.exp(line - top)
                total = total + weight
                context = context + weight * vs[j]
            e_out[i] = (context / total).astype(BF16)

    @pl.when(row == 0)
    def _():
        attend((0, 1, 2, 3))

    @pl.when(row == 1)
    def _():
        settle(d_in.at[pl.ds(0, 4), :, QUAD:], sems.at[22])
        attend((4, 5, 6, 7))

    back_copies = {}
    for k, e in enumerate((2, 1, 3)):
        to = (col + e) % 4
        back_copies[e] = remote(e_out.at[to], e_in.at[e], sems.at[25], sems.at[(26, 28, 29)[k]], (s, row * 4 + to))
        back_copies[e].start()

    def project_out(block, source):
        first = pl.multiple_of(source * QUAD, QUAD)
        return dot(block, dout[pl.ds(first, QUAD), :])

    dout_load.wait()
    result = depth_in + project_out(e_out[col], col)
    for e in (1, 3, 2):
        back_copies[e].wait_recv()
        result = result + project_out(e_in[e], (col + 4 - e) % 4)
    out_ref[...] = result.astype(BF16)

    for ref, i in (
        (look_sib, 0),
        (look_in, 2),
        (look_in, 3),
        (look_in.at[0], 5),
        (part_in.at[0], 7),
        (part_in.at[1], 8),
        (part_in.at[0], 11),
        (part_in.at[1], 12),
        (look_in, 15),
        (c_sib, 17),
        (c_in, 19),
        (d_in.at[pl.ds(0, 3)], 23),
        (e_in.at[pl.ds(0, 3)], 25),
    ):
        settle(ref, sems.at[i])

    @pl.when(row == 0)
    def _():
        settle(d_in.at[pl.ds(0, 4), :, QUAD:], sems.at[21])


def shards(
    x_resid,
    qkv_new,
    kv_cache,
    cache_lens,
    wo_temporal,
    norm_gain,
    w_in,
    embed_rows,
    token_ids,
    depth_gain,
    depth_qkv,
    depth_out,
):
    args = (
        x_resid,
        qkv_new.reshape(ROWS, (GROUP + 2) * HD),
        kv_cache.reshape(ROWS, 2, FRAMES, HD),
        cache_lens,
        wo_temporal,
        norm_gain.reshape(1, COLS),
        w_in.reshape(COLS, DDEP),
        embed_rows.reshape(128, DDEP),
        token_ids.reshape(1, 256),
        depth_gain,
        depth_qkv.reshape(DDEP, 3 * DDEP),
        depth_out.reshape(DDEP, DDEP),
    )
    args = tuple(pltpu.with_memory_space_constraint(a, pltpu.HBM) for a in args)
    dma = pltpu.SemaphoreType.DMA
    vm = pltpu.VMEM
    out = pl.pallas_call(
        frame_kernel,
        name="frame",
        out_shape=jax.ShapeDtypeStruct((ROWS, DDEP), BF16),
        in_specs=[pl.BlockSpec(memory_space=pltpu.HBM)] * len(args),
        out_specs=pl.BlockSpec(memory_space=pltpu.VMEM),
        scratch_shapes=[
            vm((ROWS, FRAMES, HD), BF16),
            vm((ROWS, FRAMES, HD), BF16),
            vm((GROUP * HD, COLS), BF16),
            vm((COLS, DDEP), BF16),
            vm((128, DDEP), BF16),
            vm((DDEP, 3 * DDEP), BF16),
            vm((DDEP, DDEP), BF16),
            vm((32, COLS), BF16),
            vm((ROWS, (GROUP + 2) * HD), BF16),
            pltpu.SMEM((ROWS,), jnp.int32),
            vm((1, COLS), F32),
            vm((1, DDEP), F32),
            vm((1, 256), jnp.int32),
            dma((6,)),
            dma((11,)),
            vm((ROWS * GROUP, HD), F32),
            vm((ROWS * GROUP, HD), F32),
            vm((ROWS * GROUP, HD), F32),
            vm((2, ROWS * HD, HD), BF16),
            vm((HD, HALF_FRAMES), F32),
            vm((ROWS * GROUP, HD), F32),
            vm((2, CHIPS, 2, ROWS, GROUP * HD // 2), BF16),
            vm((2, TP, ROWS, COLS), BF16),
            vm((2, TP - 1, ROWS, COLS), BF16),
            vm((TP, 2, ROWS, COLS), BF16),
            vm((CHIPS, 2, ROWS, 128), BF16),
            vm((CHIPS, ROWS, DDEP), BF16),
            vm((CHIPS, ROWS, DDEP), BF16),
            vm((CHIPS, ROWS, DDEP), BF16),
            vm((CHIPS, ROWS, DDEP), BF16),
            vm((CHIPS - 1, ROWS, DDEP), BF16),
            vm((CHIPS, ROWS, WIDE), BF16),
            vm((CHIPS, ROWS, WIDE), BF16),
            vm((CHIPS, ROWS, WIDE), BF16),
            vm((CHIPS - 1, ROWS, WIDE), BF16),
            vm((4, ROWS, 3 * QUAD), BF16),
            vm((TP, ROWS, 3 * QUAD), BF16),
            vm((4, ROWS, QUAD), BF16),
            vm((4, ROWS, QUAD), BF16),
            dma((14,)),
            dma((30,)),
        ],
        compiler_params=pltpu.CompilerParams(
            collective_id=0, has_side_effects=True, vmem_limit_bytes=40 * 2**20
        ),
        cost_estimate=pl.CostEstimate(flops=10**9, bytes_accessed=19 * 10**6, transcendentals=10**5),
    )(*args)
    return out.reshape(ROWS, 1, DDEP)


def solution(mesh):
    in_specs = (
        P(None, "sess"),
        P("sess", "tp", None),
        P("sess", None, "tp", None, None),
        P("sess"),
        P("tp", "sess"),
        P("sess"),
        P("tp", "sess", None),
        P("tp", "sess", None),
        P(None, "tp"),
        P("tp", None),
        P("tp", None, None),
        P("tp", None, None),
    )
    out_specs = P("sess", "tp", None)
    return jax.shard_map(shards, mesh=mesh, in_specs=in_specs, out_specs=out_specs, check_vma=False)
```
